32 devices in a mesh: facet: 2 (over y), tile: 16 (over z, x, core).
Axes of the slice: x: 2, y: 2, z: 4, core: 2. Of those that a mesh axis runs over, the one named last changes fastest.
Arguments:
- sectioned_rows: bfloat16 [2, 256, 2048], P('facet', 'tile'), may hold values from -6 to 6
- reader: int32 [16, 2], P('tile'), may hold values from 0 to 1, each once within a row
- baseline_coords: float32 [2, 2, 256], P(None, None, 'tile'), may hold values from -8 to 8
- subgrid_index: int32 [2, 256], P(None, 'tile'), may hold values from 0 to 63
- stations: int32 [2, 2, 256], P(None, None, 'tile'), may hold values from 0 to 511
- plane_index: int32 [2, 256], P(None, 'tile'), may hold values from 0 to 31
- model_grid: bfloat16 [2, 64, 2048], P('facet', 'tile'), may hold values from -0.1875 to 0.1875
- beam_screens: bfloat16 [2, 512, 2048], P('facet'), may hold values from -3.5 to 3.5
- plane_phase: float32 [32, 1024], replicated, may hold values from -3.140625 to 3.140625
- channel_freq: float32 [1024], replicated, may hold values from 0.25 to 1.75
Outputs:
- residual: float32 [2, 256, 2048], P('facet', 'tile')
- dirty_grid: float32 [2, 64, 2048], P('facet', 'tile')
The draws below stay inside these ranges and needn't reach their ends.
Inputs may be any that keep to these rules, and one draw needn't show every extreme that they name: `reader`: for each run of baselines, each facet group read exactly one block.
All inputs are finite; a program needn't handle non-finite values.
Results may differ from the reference program's by a relative error of at most 0.0033.
Values may be sent and summed in bfloat16 or wider, within the bound.
A program may use at most 128 MiB of HBM per device.

```python
import math
import jax
import jax.numpy as jnp
import numpy as np
from jax import lax

EDGE = 32
PIXELS = 1024
CHANNELS = 1024
STATIONS = 512
PLANES = 32
ROW_DEV = 16
BLOCKS = 2
FACETS = 2
ROWS = 256
SUBGRIDS = 64
N_TILE = 16


def corner_factor():
    cell_ids = jnp.arange(PIXELS, dtype=jnp.int32)
    row_offset = cell_ids // EDGE - EDGE // 2
    col_offset = cell_ids % EDGE - EDGE // 2
    distance = jnp.abs(row_offset) + jnp.abs(col_offset)
    return jnp.where(distance >= 3 * EDGE // 4, 1.0, 0.25).astype(jnp.float32)


def draw_beam_screens(key, part):
    key = jax.random.fold_in(key, 11)
    factor = corner_factor()
    factor = jnp.concatenate([factor, factor])
    values = jnp.clip(0.7 * jax.random.normal(key, (FACETS, STATIONS, 2 * PIXELS), jnp.float32), -3.5, 3.5)
    return (values * factor[None, None, :]).astype(jnp.bfloat16)


def draw_baseline_coords(key, part):
    key = jax.random.fold_in(key, 7)
    sign_key, size_key = jax.random.split(key)
    sign_pick = (2 * jax.random.randint(sign_key, (BLOCKS, 2, ROWS), 0, 2) - 1).astype(jnp.float32)
    magnitude = jax.random.uniform(size_key, (BLOCKS, 2, ROWS), jnp.float32, 6.0, 8.0)
    return (sign_pick * magnitude).astype(jnp.float32)


def set_ends(drawn, rng, least, top_value):
    dims = drawn.shape
    index_at = [jax.random.randint(jax.random.fold_in(rng, axis), (), 0, dims[axis]) for axis in range(len(dims))]
    drawn = drawn.at[tuple(index_at)].set(least)
    longest = dims.index(max(dims))
    index_at[longest] = (index_at[longest] + 1) % dims[longest]
    return drawn.at[tuple(index_at)].set(top_value)


def shard_levels(stream_key, extent, cuts, smallest, top_value):
    gain, own = 1.0, jax.random.fold_in(stream_key, 6)
    for axis_at, shards_of in cuts:
        heights = jnp.exp(jax.random.uniform(jax.random.fold_in(own, axis_at), (shards_of,), jnp.float32, smallest / len(cuts), top_value / len(cuts)))
        gain = gain * jnp.repeat(heights, extent[axis_at] // shards_of).reshape([-1 if axis == axis_at else 1 for axis in range(len(extent))])
    return gain


def cumulative_ranks(amount, slope):
    portions = [(1 << 20) // math.isqrt(standing ** slope) + 1 for standing in range(1, amount + 1)]
    scale = 1 + sum(portions) // (1 << 30)
    return np.cumsum(np.array([max(1, weight // scale) for weight in portions]))


def skewed_ids(rng, shape, amount, slope):
    grid = cumulative_ranks(amount, slope)
    ticket = jax.random.randint(jax.random.fold_in(rng, 1), shape, 0, int(grid[amount - 1]))
    standing = jnp.searchsorted(jnp.asarray(grid, jnp.int32), ticket, side="right")
    return jax.random.permutation(jax.random.fold_in(rng, 2), amount)[standing].astype(jnp.int32)


def scatter_about(rng, shape, width, most, cuts=(), held_as=jnp.bfloat16):
    level = shard_levels(rng, shape, cuts, -0.22, 0.18) if cuts else 1.0
    values = jax.random.normal(rng, shape, jnp.float32) * width * level
    return jnp.minimum(jnp.maximum(values, -most), most).astype(held_as)


def setup_inputs(seed: int = 0) -> dict:
    key_list = jax.random.split(jax.random.key(seed), 11)
    return {
        "sectioned_rows": scatter_about(key_list[0], (BLOCKS, ROWS, 2 * CHANNELS), 1.0, 6.0, ((0, 2), (1, 16))),
        "reader": jax.vmap(lambda own: jax.random.permutation(own, BLOCKS))(jax.random.split(key_list[1], N_TILE)).reshape((N_TILE, BLOCKS)).astype(jnp.int32),
        "baseline_coords": draw_baseline_coords(jax.random.fold_in(key_list[10], 71), 0),
        "subgrid_index": set_ends(skewed_ids(key_list[3], (BLOCKS, ROWS), SUBGRIDS, 2), jax.random.fold_in(key_list[3], 3), 0, SUBGRIDS - 1).astype(jnp.int32),
        "stations": set_ends(jax.random.randint(key_list[4], (BLOCKS, 2, ROWS), 0, STATIONS), jax.random.fold_in(key_list[4], 1), 0, STATIONS - 1).astype(jnp.int32),
        "plane_index": set_ends(jax.random.randint(key_list[5], (BLOCKS, ROWS), 0, PLANES), jax.random.fold_in(key_list[5], 1), 0, PLANES - 1).astype(jnp.int32),
        "model_grid": scatter_about(key_list[6], (FACETS, SUBGRIDS, 2 * PIXELS), PIXELS ** -0.5, 0.1875, ((0, 2), (1, 16))),
        "beam_screens": draw_beam_screens(jax.random.fold_in(key_list[10], 71), 0),
        "plane_phase": jnp.clip(jax.random.uniform(key_list[8], (PLANES, PIXELS), jnp.float32, -3.140625, 3.140625), -3.140625, 3.140625),
        "channel_freq": jnp.clip(jax.random.uniform(key_list[9], (CHANNELS,), jnp.float32, 0.25, 1.75), 0.25, 1.75),
    }


TWO_PI = 2.0 * math.pi

def phasor_tables(coords, channel_freq, edge_cells):
    offsets = (jnp.arange(edge_cells, dtype=jnp.float32) - edge_cells // 2) / edge_cells
    angles = TWO_PI * coords[:, None, None] * offsets[None, :, None] * channel_freq[None, None, :]
    return (jnp.cos(angles).astype(jnp.bfloat16), jnp.sin(angles).astype(jnp.bfloat16))

def north_matrix(north_cos, north_sin):
    upper_half = jnp.concatenate([north_cos, north_sin], axis=2)
    lower_half = jnp.concatenate([-north_sin, north_cos], axis=2)
    return jnp.concatenate([upper_half, lower_half], axis=1)

def screen_parts(screens, station_pair, plane_rows, plane_phase):
    pixels = plane_phase.shape[1]
    station_one = screens[station_pair[0]].astype(jnp.float32)
    station_two = screens[station_pair[1]].astype(jnp.float32)
    one_re, one_im = (station_one[:, :pixels], station_one[:, pixels:])
    two_re, two_im = (station_two[:, :pixels], station_two[:, pixels:])
    pair_re = one_re * two_re + one_im * two_im
    pair_im = one_im * two_re - one_re * two_im
    angles = plane_phase[plane_rows]
    wave_re, wave_im = (jnp.cos(angles), jnp.sin(angles))
    return (pair_re * wave_re - pair_im * wave_im, pair_re * wave_im + pair_im * wave_re)

def degrid_rows(model_rows, screen_re, screen_im, east_cos, east_sin, north_mat):
    row_count = model_rows.shape[0]
    pixels = model_rows.shape[1] // 2
    edge_cells = east_cos.shape[1]
    channels = east_cos.shape[2]
    model_f = model_rows.astype(jnp.float32)
    model_re, model_im = (model_f[:, :pixels], model_f[:, pixels:])
    image_re = screen_re * model_re - screen_im * model_im
    image_im = screen_re * model_im + screen_im * model_re
    operand = jnp.concatenate([image_re.reshape(row_count, edge_cells, edge_cells), image_im.reshape(row_count, edge_cells, edge_cells)], axis=2).astype(jnp.bfloat16)
    inner_sum = jnp.einsum('rxy,ryc->rxc', operand.astype(jnp.float32), north_mat.astype(jnp.float32))
    inner_re, inner_im = (inner_sum[:, :, :channels], inner_sum[:, :, channels:])
    cos_f, sin_f = (east_cos.astype(jnp.float32), east_sin.astype(jnp.float32))
    vis_re = lax.optimization_barrier(jnp.sum(cos_f * inner_re - sin_f * inner_im, axis=1))
    vis_im = lax.optimization_barrier(jnp.sum(cos_f * inner_im + sin_f * inner_re, axis=1))
    return jnp.concatenate([vis_re, vis_im], axis=1)

def grid_rows(resid_rows, screen_re, screen_im, east_cos, east_sin, north_mat, grid_scale):
    row_count = resid_rows.shape[0]
    edge_cells = east_cos.shape[1]
    channels = east_cos.shape[2]
    resid_f = resid_rows.astype(jnp.float32)
    resid_re, resid_im = (resid_f[:, None, :channels], resid_f[:, None, channels:])
    cos_f, sin_f = (east_cos.astype(jnp.float32), east_sin.astype(jnp.float32))
    weighted_re = cos_f * resid_re + sin_f * resid_im
    weighted_im = cos_f * resid_im - sin_f * resid_re
    operand = jnp.concatenate([weighted_re, weighted_im], axis=2).astype(jnp.bfloat16)
    gridded = jnp.einsum('rxc,ryc->rxy', operand.astype(jnp.float32), north_mat.astype(jnp.float32))
    grid_re = gridded[:, :, :edge_cells].reshape(row_count, edge_cells * edge_cells)
    grid_im = gridded[:, :, edge_cells:].reshape(row_count, edge_cells * edge_cells)
    out_re = (screen_re * grid_re + screen_im * grid_im) * grid_scale
    out_im = (screen_re * grid_im - screen_im * grid_re) * grid_scale
    return jnp.concatenate([out_re, out_im], axis=1).astype(jnp.bfloat16)

def reference(sectioned_rows, reader, baseline_coords, subgrid_index, stations, plane_index, model_grid, beam_screens, plane_phase, channel_freq):
    sectioned_runs = sectioned_rows.reshape(BLOCKS, N_TILE, ROW_DEV, 2 * CHANNELS)
    run_ids = jnp.arange(N_TILE, dtype=jnp.int32)
    visible = sectioned_runs[reader.T, run_ids[None, :]].reshape(BLOCKS, ROWS, 2 * CHANNELS)
    grid_scale = 1.0 / math.sqrt(CHANNELS * BLOCKS * ROWS / SUBGRIDS)
    targets = jnp.arange(SUBGRIDS, dtype=jnp.int32)

    def per_block(block_id):
        east_cos, east_sin = phasor_tables(baseline_coords[block_id, 0], channel_freq, EDGE)
        north_cos, north_sin = phasor_tables(baseline_coords[block_id, 1], channel_freq, EDGE)
        north_mat = north_matrix(north_cos, north_sin)
        rows_sub = subgrid_index[block_id]
        screens_all = [screen_parts(beam_screens[facet_id], stations[block_id], plane_index[block_id], plane_phase) for facet_id in range(FACETS)]
        predicted = jnp.zeros((ROWS, 2 * CHANNELS), jnp.float32)
        for facet_id in range(FACETS):
            screen_re, screen_im = screens_all[facet_id]
            predicted = predicted + degrid_rows(model_grid[facet_id][rows_sub], screen_re, screen_im, east_cos, east_sin, north_mat)
        resid_block = visible[block_id].astype(jnp.float32) - predicted
        onehot = (targets[:, None] == rows_sub[None, :]).astype(jnp.bfloat16)
        partials = []
        for facet_id in range(FACETS):
            screen_re, screen_im = screens_all[facet_id]
            regridded = grid_rows(resid_block, screen_re, screen_im, east_cos, east_sin, north_mat, grid_scale)
            partials.append(jnp.dot(onehot, regridded, preferred_element_type=jnp.float32))
        return (resid_block, jnp.stack(partials))
    residual, partials = lax.map(per_block, jnp.arange(BLOCKS, dtype=jnp.int32))
    return (residual, lax.optimization_barrier(jnp.sum(partials, axis=0)))
```

```python
import functools
import math

import jax
import jax.numpy as jnp
from jax import lax
from jax.experimental import pallas as pl
from jax.experimental.pallas import tpu as pltpu
from jax.sharding import PartitionSpec as P

MESH = pl.DeviceIdType.MESH
F32 = jnp.float32
BF16 = jnp.bfloat16


def cos_sin(x):
    y = x * x
    c = 1.0 / math.factorial(12)
    s = 1.0 / math.factorial(13)
    for k in range(5, -1, -1):
        sign = -1.0 if k % 2 else 1.0
        c = c * y + sign / math.factorial(2 * k)
        s = s * y + sign / math.factorial(2 * k + 1)
    return c, s * x


def iota(shape, dim):
    return lax.broadcasted_iota(jnp.int32, shape, dim)


def fold_values(cell, part_col):
    k = part_col % 16
    odd = part_col // 16
    hit = (cell == 16 + k).astype(F32)
    other = (cell == 15 - k).astype(F32)
    value = hit + other * (1.0 - 2.0 * odd.astype(F32))
    return jnp.where(part_col < 32, value, 0.0).astype(BF16)


def kernel(
    n_facet, n_tile, owned, run, channels, grid_scale,
    reader_ref, cols_ref, index_ref, index_col_ref, index_row_ref,
    rows_ref, model_ref, screens_hbm, phase_ref, freq_ref,
    resid_ref, dirty_ref,
    screens, model_send, model_all, arrived, pred_send, pred_all, part_send, part_all,
    te, tn, mats, hre, him, vre, vim, sre, sim,
    local_sem, model_ss, model_rs, vis_ss, vis_rs, pred_ss, pred_rs, part_ss, part_rs,
):
    R = n_facet * run
    me_f = lax.axis_index("facet")
    me_t = lax.axis_index("tile")
    chunk = model_send.shape[0]
    quarter = model_send.shape[1]

    load = pltpu.make_async_copy(screens_hbm, screens, local_sem)
    load.start()

    def tile_peer(p):
        return lax.rem(me_t + p, n_tile)

    def facet_peer(p):
        return lax.rem(me_f + p, n_facet)

    barrier = pltpu.get_barrier_semaphore()

    def greet_tile(p, c):
        pl.semaphore_signal(barrier, inc=1, device_id=(me_f, tile_peer(p)), device_id_type=MESH)
        return c

    def greet_facet(p, c):
        pl.semaphore_signal(barrier, inc=1, device_id=(facet_peer(p), me_t), device_id_type=MESH)
        return c

    lax.fori_loop(1, n_tile, greet_tile, 0)
    lax.fori_loop(1, n_facet, greet_facet, 0)

    model_f = model_ref[0].astype(F32)
    model_send[...] = jnp.concatenate(
        [model_f[:, q * quarter:(q + 1) * quarter] for q in range(4)], axis=0
    ).astype(BF16)
    pl.semaphore_wait(barrier, n_tile + n_facet - 2)

    def model_copy(o, slot):
        return pltpu.make_async_remote_copy(
            src_ref=model_send, dst_ref=model_all.at[slot], send_sem=model_ss.at[o],
            recv_sem=model_rs.at[slot], device_id=(me_f, o), device_id_type=MESH)

    def vis_copy(o, slot):
        return pltpu.make_async_remote_copy(
            src_ref=rows_ref.at[0], dst_ref=arrived.at[slot], send_sem=vis_ss.at[o],
            recv_sem=vis_rs.at[slot], device_id=(o, me_t), device_id_type=MESH)

    def pred_copy(o, slot, k):
        return pltpu.make_async_remote_copy(
            src_ref=pred_send.at[k], dst_ref=pred_all.at[slot, k], send_sem=pred_ss.at[o, k],
            recv_sem=pred_rs.at[slot, k], device_id=(o, me_t), device_id_type=MESH)

    def part_copy(o, slot):
        return pltpu.make_async_remote_copy(
            src_ref=part_send.at[o], dst_ref=part_all.at[slot], send_sem=part_ss.at[o],
            recv_sem=part_rs.at[slot], device_id=(me_f, o), device_id_type=MESH)

    def send_model(p, c):
        model_copy(tile_peer(p), me_t).start()
        return c

    def send_vis(p, c):
        vis_copy(facet_peer(p), me_f).start()
        return c

    lax.fori_loop(1, n_tile, send_model, 0)
    lax.fori_loop(1, n_facet, send_vis, 0)
    model_all[me_t] = model_send[...]
    arrived[me_f] = rows_ref[0]

    def tables(g, c):
        r0 = pl.multiple_of(g * 8, 8)
        freq = freq_ref[...]
        halves = []
        for col, dst in ((0, te), (1, tn)):
            u = cols_ref[pl.ds(r0, 8), col:col + 1]
            alpha = (u * (2.0 * math.pi / 64.0)) * freq
            c0, s0 = cos_sin(alpha)
            halves.append((c0, s0))
            twice = 2.0 - 4.0 * s0 * s0
            c_old, s_old, c_now, s_now = c0, -s0, c0, s0
            for j in range(16):
                for b in range(channels // 128):
                    lanes = slice(128 * b, 128 * b + 128)
                    dst[b, pl.ds(r0 * 32 + j, 8, stride=32), :] = c_now[:, lanes]
                    dst[b, pl.ds(r0 * 32 + 16 + j, 8, stride=32), :] = s_now[:, lanes]
                if j < 15:
                    c_old, c_now = c_now, twice * c_now - c_old
                    s_old, s_now = s_now, twice * s_now - s_old
        (ca, sa), (cb, sb) = halves
        hre[pl.ds(r0, 8), :] = ca * cb - sa * sb
        him[pl.ds(r0, 8), :] = ca * sb + sa * cb
        return c

    lax.fori_loop(0, R // 8, tables, 0)

    stations = screens.shape[0]
    planes, pixels = phase_ref.shape
    half_c, half_s = cos_sin(phase_ref[...] * 0.5)
    waves = jnp.concatenate([1.0 - 2.0 * half_s * half_s, 2.0 * half_s * half_c], axis=1)
    plane_hot = (index_ref[:, 2:3] == iota((R, planes), 1)).astype(F32)
    wave = jnp.dot(plane_hot, waves, preferred_element_type=F32, precision=lax.Precision.HIGHEST)
    wave_re, wave_im = wave[:, :pixels], wave[:, pixels:]
    load.wait()
    one_hot = (index_ref[:, 0:1] == iota((R, stations), 1)).astype(F32).astype(BF16)
    two_hot = (index_ref[:, 1:2] == iota((R, stations), 1)).astype(F32).astype(BF16)
    one = jnp.dot(one_hot, screens[...], preferred_element_type=F32)
    two = jnp.dot(two_hot, screens[...], preferred_element_type=F32)
    one_re, one_im, two_re, two_im = one[:, :pixels], one[:, pixels:], two[:, :pixels], two[:, pixels:]
    pair_re = one_re * two_re + one_im * two_im
    pair_im = one_im * two_re - one_re * two_im
    sre[...] = pair_re * wave_re - pair_im * wave_im
    sim[...] = pair_re * wave_im + pair_im * wave_re

    def wait_model(p, c):
        o = tile_peer(p)
        model_copy(o, o).wait()
        return c

    lax.fori_loop(1, n_tile, wait_model, 0)
    total = n_tile * chunk
    own_i = iota((4 * R, total), 1)
    pick = (index_col_ref[...] == (own_i // chunk) * owned + own_i % owned) & (
        (own_i // owned) % 4 == iota((4 * R, total), 0) // R)
    found = jnp.dot(pick.astype(F32).astype(BF16), model_all[...].reshape(total, quarter),
                    preferred_element_type=F32)
    model_re = jnp.concatenate([found[:R], found[R:2 * R]], axis=1)
    model_im = jnp.concatenate([found[2 * R:3 * R], found[3 * R:]], axis=1)
    image = jnp.concatenate(
        [sre[...] * model_re - sim[...] * model_im, sre[...] * model_im + sim[...] * model_re], axis=0
    ).astype(BF16)

    fr, fc = iota((128, 512), 0), iota((128, 512), 1)
    fold = jnp.where(fr // 32 == fc // 128, fold_values(fr % 32, fc % 128).astype(F32), 0.0).astype(BF16)
    low = iota((R, 128), 1) < 16
    by_x = {}
    for g in range(8):
        got = jnp.dot(image[:, 128 * g:128 * g + 128], fold, preferred_element_type=F32)
        for i in range(4):
            by_x[4 * g + i] = got[:, 128 * i:128 * i + 128]
    for j in range(16):
        up, down = by_x[16 + j], by_x[15 - j]
        even, odd = up + down, up - down
        e_re, e_im, o_re, o_im = even[:R], even[R:], odd[:R], odd[R:]
        parts = (jnp.where(low, e_re, -e_im), -jnp.where(low, o_im, o_re),
                 jnp.where(low, e_im, e_re), jnp.where(low, o_re, -o_im))
        for q in range(4):
            mats[(q * 16 + j) * R:(q * 16 + j + 1) * R, :] = parts[q]

    step = 256

    def table(ref, at, lo):
        return jnp.concatenate([ref[lo // 128 + b, pl.ds(at, 32), :] for b in range(step // 128)], axis=1)

    def degrid(r):
        lhs = mats[pl.ds(r, 64, stride=R), :][:, :32].astype(BF16)
        at = pl.multiple_of(r * 32, 32)
        for lo in range(0, channels, step):
            inner = jnp.dot(lhs, table(tn, at, lo).astype(BF16), preferred_element_type=F32)
            east = table(te, at, lo)
            vre[pl.ds(r, 1), lo:lo + step] = jnp.sum(east * inner[:32], axis=0, keepdims=True)
            vim[pl.ds(r, 1), lo:lo + step] = jnp.sum(east * inner[32:], axis=0, keepdims=True)

    def predict(k, c):
        def pair(i, d):
            degrid(k * run + 2 * i)
            degrid(k * run + 2 * i + 1)
            return d

        lax.fori_loop(0, run // 2, pair, 0)
        r0 = pl.multiple_of(k * run, run)
        a_re, a_im = vre[pl.ds(r0, run), :], vim[pl.ds(r0, run), :]
        h_re, h_im = hre[pl.ds(r0, run), :], him[pl.ds(r0, run), :]
        p_re = a_re * h_re + a_im * h_im
        p_im = a_im * h_re - a_re * h_im
        vre[pl.ds(r0, run), :] = p_re
        vim[pl.ds(r0, run), :] = p_im
        pred_send[k, :, :channels] = p_re.astype(BF16)
        pred_send[k, :, channels:] = p_im.astype(BF16)

        def send_pred(p, d):
            pred_copy(facet_peer(p), me_f, k).start()
            return d

        lax.fori_loop(1, n_facet, send_pred, 0)
        return c

    lax.fori_loop(0, n_facet, predict, 0)

    def wait_vis(p, c):
        o = facet_peer(p)
        vis_copy(o, o).wait()
        return c

    lax.fori_loop(1, n_facet, wait_vis, 0)

    def regrid(r):
        at = pl.multiple_of(r * 32, 32)
        acc = jnp.zeros((64, 32), F32)
        for lo in range(0, channels, step):
            east = table(te, at, lo)
            weighted = jnp.concatenate(
                [east * vre[pl.ds(r, 1), lo:lo + step], east * vim[pl.ds(r, 1), lo:lo + step]], axis=0
            ).astype(BF16)
            acc = acc + lax.dot_general(
                weighted, table(tn, at, lo).astype(BF16),
                (((1,), (1,)), ((), ())), preferred_element_type=F32)
        mats[pl.ds(r, 64, stride=R), :] = jnp.concatenate([acc, jnp.zeros((64, 96), F32)], axis=1)

    def grid_block(k, c):
        r0 = pl.multiple_of(k * run, run)

        def wait_pred(p, d):
            o = facet_peer(p)
            pred_copy(o, o, k).wait()
            return d

        lax.fori_loop(1, n_facet, wait_pred, 0)
        res_re = -vre[pl.ds(r0, run), :]
        res_im = -vim[pl.ds(r0, run), :]
        for p in range(1, n_facet):
            other = pred_all[facet_peer(p), k].astype(F32)
            res_re = res_re - other[:, :channels]
            res_im = res_im - other[:, channels:]
        for g in range(n_facet):
            share = (reader_ref[0, k] == g).astype(F32)
            seen = arrived[g].astype(F32) * share
            res_re = res_re + seen[:, :channels]
            res_im = res_im + seen[:, channels:]

        @pl.when(k == me_f)
        def _():
            resid_ref[0, :, :channels] = res_re
            resid_ref[0, :, channels:] = res_im

        h_re, h_im = hre[pl.ds(r0, run), :], him[pl.ds(r0, run), :]
        vre[pl.ds(r0, run), :] = res_re * h_re - res_im * h_im
        vim[pl.ds(r0, run), :] = res_re * h_im + res_im * h_re

        def pair(i, d):
            regrid(k * run + 2 * i)
            regrid(k * run + 2 * i + 1)
            return d

        lax.fori_loop(0, run // 2, pair, 0)
        return c

    lax.fori_loop(0, n_facet, grid_block, 0)

    ur, uc = iota((512, 128), 0), iota((512, 128), 1)
    unfold = jnp.where(ur // 128 == uc // 32, fold_values(uc % 32, ur % 128).astype(F32), 0.0).astype(BF16)
    spread = {}
    for j in range(16):
        c_re, s_re, c_im, s_im = (mats[(q * 16 + j) * R:(q * 16 + j + 1) * R, :] for q in range(4))
        for x, sign in ((16 + j, 1.0), (15 - j, -1.0)):
            m = c_re + sign * s_im
            n = c_im - sign * s_re
            spread[x] = jnp.concatenate([jnp.where(low, m, n), jnp.where(low, n, -m)], axis=0).astype(BF16)
    out_re, out_im = [], []
    for g in range(8):
        cells = jnp.dot(jnp.concatenate([spread[4 * g + i] for i in range(4)], axis=1), unfold,
                        preferred_element_type=F32)
        g_re, g_im = cells[:R], cells[R:]
        s_re, s_im = sre[:, 128 * g:128 * g + 128], sim[:, 128 * g:128 * g + 128]
        out_re.append(((s_re * g_re + s_im * g_im) * grid_scale).astype(BF16))
        out_im.append(((s_re * g_im - s_im * g_re) * grid_scale).astype(BF16))
    both = out_re + out_im
    stacked = jnp.concatenate(
        [jnp.concatenate(both[4 * q:4 * q + 4], axis=1) for q in range(4)], axis=0)
    own_r = iota((total, 4 * R), 0)
    place = (index_row_ref[...] == (own_r // chunk) * owned + own_r % owned) & (
        (own_r // owned) % 4 == iota((total, 4 * R), 1) // R)
    sums = jnp.dot(place.astype(F32).astype(BF16), stacked, preferred_element_type=F32)
    part_send[...] = sums.astype(BF16).reshape(n_tile, chunk, quarter)

    def send_part(p, c):
        part_copy(tile_peer(p), me_t).start()
        return c

    lax.fori_loop(1, n_tile, send_part, 0)

    def add_part(p, acc):
        o = tile_peer(p)
        part_copy(o, o).wait()
        return acc + part_all[o].astype(F32)

    acc = lax.fori_loop(1, n_tile, add_part, part_send[me_t].astype(F32))
    for q in range(4):
        dirty_ref[0, :, q * quarter:(q + 1) * quarter] = acc[q * owned:(q + 1) * owned]


def local(
    sectioned_rows,
    reader,
    baseline_coords,
    subgrid_index,
    stations,
    plane_index,
    model_grid,
    beam_screens,
    plane_phase,
    channel_freq,
):
    n_facet = lax.axis_size("facet")
    n_tile = lax.axis_size("tile")
    channels = channel_freq.shape[0]
    pixels = plane_phase.shape[1]
    run = sectioned_rows.shape[1]
    owned = model_grid.shape[1]
    R = n_facet * run
    chunk, quarter = 4 * owned, 2 * pixels // 4
    grid_scale = 1.0 / math.sqrt(channels * n_facet * (run * n_tile) / (owned * n_tile))

    cols = jnp.stack([baseline_coords[:, 0].reshape(R), baseline_coords[:, 1].reshape(R)], axis=1)
    index = jnp.stack(
        [stations[:, 0].reshape(R), stations[:, 1].reshape(R), plane_index.reshape(R)], axis=1)
    flat = jnp.tile(subgrid_index.reshape(R), 4)

    vmem = pl.BlockSpec(memory_space=pltpu.VMEM)
    body = functools.partial(kernel, n_facet, n_tile, owned, run, channels, grid_scale)
    dma = pltpu.SemaphoreType.DMA
    resid, dirty = pl.pallas_call(
        body,
        out_shape=(
            jax.ShapeDtypeStruct((1, run, 2 * channels), F32),
            jax.ShapeDtypeStruct((1, owned, 2 * pixels), F32),
        ),
        in_specs=[pl.BlockSpec(memory_space=pltpu.SMEM)] + [vmem] * 6
        + [pl.BlockSpec(memory_space=pl.ANY)] + [vmem] * 2,
        out_specs=(vmem, vmem),
        scratch_shapes=[
            pltpu.VMEM(beam_screens.shape[1:], BF16),
            pltpu.VMEM((chunk, quarter), BF16),
            pltpu.VMEM((n_tile, chunk, quarter), BF16),
            pltpu.VMEM((n_facet, run, 2 * channels), BF16),
            pltpu.VMEM((n_facet, run, 2 * channels), BF16),
            pltpu.VMEM((n_facet, n_facet, run, 2 * channels), BF16),
            pltpu.VMEM((n_tile, chunk, quarter), BF16),
            pltpu.VMEM((n_tile, chunk, quarter), BF16),
            pltpu.VMEM((channels // 128, R * 32, 128), F32),
            pltpu.VMEM((channels // 128, R * 32, 128), F32),
            pltpu.VMEM((64 * R, 128), F32),
            pltpu.VMEM((R, channels), F32),
            pltpu.VMEM((R, channels), F32),
            pltpu.VMEM((R, channels), F32),
            pltpu.VMEM((R, channels), F32),
            pltpu.VMEM((R, pixels), F32),
            pltpu.VMEM((R, pixels), F32),
            dma,
            dma((n_tile,)), dma((n_tile,)),
            dma((n_facet,)), dma((n_facet,)),
            dma((n_facet, n_facet)), dma((n_facet, n_facet)),
            dma((n_tile,)), dma((n_tile,)),
        ],
        compiler_params=pltpu.CompilerParams(
            collective_id=0, has_side_effects=True, vmem_limit_bytes=60 * 1024 * 1024),
        name="predict_regrid",
    )(reader, cols, index, flat[:, None], flat[None, :], sectioned_rows, model_grid,
      beam_screens[0], plane_phase, channel_freq[None, :])
    return (resid, dirty)


def solution(mesh):
    return jax.shard_map(
        local,
        mesh=mesh,
        in_specs=(
            P("facet", "tile", None),
            P("tile", None),
            P(None, None, "tile"),
            P(None, "tile"),
            P(None, None, "tile"),
            P(None, "tile"),
            P("facet", "tile", None),
            P("facet", None, None),
            P(),
            P(),
        ),
        out_specs=(P("facet", "tile", None), P("facet", "tile", None)),
        check_vma=False,
    )
```

```python
import functools
import math

import jax
import jax.numpy as jnp
from jax import lax
from jax.experimental import pallas as pl
from jax.experimental.pallas import tpu as pltpu
from jax.sharding import PartitionSpec as P

MESH = pl.DeviceIdType.MESH
F32 = jnp.float32
BF16 = jnp.bfloat16


def cos_sin(x):
    y = x * x
    c = 1.0 / math.factorial(12)
    s = 1.0 / math.factorial(13)
    for k in range(5, -1, -1):
        sign = -1.0 if k % 2 else 1.0
        c = c * y + sign / math.factorial(2 * k)
        s = s * y + sign / math.factorial(2 * k + 1)
    return c, s * x


def iota(shape, dim):
    return lax.broadcasted_iota(jnp.int32, shape, dim)


def fold_values(cell, part_col):
    k = part_col % 16
    odd = part_col // 16
    hit = (cell == 16 + k).astype(F32)
    other = (cell == 15 - k).astype(F32)
    value = hit + other * (1.0 - 2.0 * odd.astype(F32))
    return jnp.where(part_col < 32, value, 0.0).astype(BF16)


def column(rows):
    n = rows[0].shape[1]
    diagonal = iota((n, n), 0) == iota((n, n), 1)
    return jnp.concatenate(
        [jnp.sum(jnp.where(diagonal, row.astype(F32), 0.0), axis=1, keepdims=True) for row in rows], axis=0)


def kernel(
    n_facet, n_tile, owned, run, channels, grid_scale,
    reader_ref, coords_ref, subgrid_ref, stations_ref, plane_ref, rows_ref, model_ref, screens_hbm, phase_ref, freq_ref,
    resid_ref, dirty_ref,
    cols, screens, model_send, model_all, arrived, pred_send, pred_all, part_send, part_all,
    te, tn, mats, hre, him, vre, vim, sre, sim,
    local_sem, model_ss, model_rs, vis_ss, vis_rs, pred_ss, pred_rs, part_ss, part_rs,
):
    R = n_facet * run
    me_f = lax.axis_index("facet")
    me_t = lax.axis_index("tile")
    chunk = model_send.shape[0]
    quarter = model_send.shape[1]

    load = pltpu.make_async_copy(screens_hbm, screens, local_sem)
    load.start()

    def tile_peer(p):
        return lax.rem(me_t + p, n_tile)

    def facet_peer(p):
        return lax.rem(me_f + p, n_facet)

    barrier = pltpu.get_barrier_semaphore()

    def greet_tile(p, c):
        pl.semaphore_signal(barrier, inc=1, device_id=(me_f, tile_peer(p)), device_id_type=MESH)
        return c

    def greet_facet(p, c):
        pl.semaphore_signal(barrier, inc=1, device_id=(facet_peer(p), me_t), device_id_type=MESH)
        return c

    lax.fori_loop(1, n_tile, greet_tile, 0)
    lax.fori_loop(1, n_facet, greet_facet, 0)

    model_f = model_ref[0].astype(F32)
    model_send[...] = jnp.concatenate(
        [model_f[:, q * quarter:(q + 1) * quarter] for q in range(4)], axis=0
    ).astype(BF16)
    for axis in range(2):
        cols[:, axis:axis + 1] = column([coords_ref[k, axis:axis + 1, :] for k in range(n_facet)])

    def tables(axis, dst):
        def group(g, c):
            r0 = pl.multiple_of(g * 8, 8)
            alpha = (cols[pl.ds(r0, 8), axis:axis + 1] * (2.0 * math.pi / 64.0)) * freq_ref[...]
            c0, s0 = cos_sin(alpha)
            twice = 2.0 - 4.0 * s0 * s0
            c_old, s_old, c_now, s_now = c0, -s0, c0, s0
            for j in range(16):
                for b in range(channels // 128):
                    lanes = slice(128 * b, 128 * b + 128)
                    dst[b, pl.ds(r0 * 32 + j, 8, stride=32), :] = c_now[:, lanes]
                    dst[b, pl.ds(r0 * 32 + 16 + j, 8, stride=32), :] = s_now[:, lanes]
                if j < 15:
                    c_old, c_now = c_now, twice * c_now - c_old
                    s_old, s_now = s_now, twice * s_now - s_old
            if axis == 0:
                hre[pl.ds(r0, 8), :] = c0
                him[pl.ds(r0, 8), :] = s0
            else:
                ca, sa = hre[pl.ds(r0, 8), :], him[pl.ds(r0, 8), :]
                hre[pl.ds(r0, 8), :] = ca * c0 - sa * s0
                him[pl.ds(r0, 8), :] = ca * s0 + sa * c0
            return c

        lax.fori_loop(0, R // 8, group, 0)

    tables(0, te)
    pl.semaphore_wait(barrier, n_tile + n_facet - 2)

    def model_copy(o, slot):
        return pltpu.make_async_remote_copy(
            src_ref=model_send, dst_ref=model_all.at[slot], send_sem=model_ss.at[o],
            recv_sem=model_rs.at[slot], device_id=(me_f, o), device_id_type=MESH)

    def vis_copy(o, slot):
        return pltpu.make_async_remote_copy(
            src_ref=rows_ref.at[0], dst_ref=arrived.at[slot], send_sem=vis_ss.at[o],
            recv_sem=vis_rs.at[slot], device_id=(o, me_t), device_id_type=MESH)

    def pred_copy(o, slot, k):
        return pltpu.make_async_remote_copy(
            src_ref=pred_send.at[k], dst_ref=pred_all.at[slot, k], send_sem=pred_ss.at[o, k],
            recv_sem=pred_rs.at[slot, k], device_id=(o, me_t), device_id_type=MESH)

    def part_copy(o, slot):
        return pltpu.make_async_remote_copy(
            src_ref=part_send.at[o], dst_ref=part_all.at[slot], send_sem=part_ss.at[o],
            recv_sem=part_rs.at[slot], device_id=(me_f, o), device_id_type=MESH)

    def send_model(p, c):
        model_copy(tile_peer(p), me_t).start()
        return c

    def send_vis(p, c):
        vis_copy(facet_peer(p), me_f).start()
        return c

    lax.fori_loop(1, n_tile, send_model, 0)
    lax.fori_loop(1, n_facet, send_vis, 0)
    model_all[me_t] = model_send[...]
    arrived[me_f] = rows_ref[0]

    tables(1, tn)

    stations = screens.shape[0]
    planes, pixels = phase_ref.shape
    half_c, half_s = cos_sin(phase_ref[...] * 0.5)
    waves = jnp.concatenate([1.0 - 2.0 * half_s * half_s, 2.0 * half_s * half_c], axis=1)
    plane_hot = (column([plane_ref[k:k + 1, :] for k in range(n_facet)]) == iota((R, planes), 1).astype(F32)).astype(F32)
    wave = jnp.dot(plane_hot, waves, preferred_element_type=F32, precision=lax.Precision.HIGHEST)
    wave_re, wave_im = wave[:, :pixels], wave[:, pixels:]
    load.wait()
    pair_col = column([stations_ref[k, a:a + 1, :] for a in range(2) for k in range(n_facet)])
    station_hot = (pair_col == iota((2 * R, stations), 1).astype(F32)).astype(F32).astype(BF16)
    both_rows = jnp.dot(station_hot, screens[...], preferred_element_type=F32)
    one, two = both_rows[:R], both_rows[R:]
    one_re, one_im, two_re, two_im = one[:, :pixels], one[:, pixels:], two[:, :pixels], two[:, pixels:]
    pair_re = one_re * two_re + one_im * two_im
    pair_im = one_im * two_re - one_re * two_im
    sre[...] = pair_re * wave_re - pair_im * wave_im
    sim[...] = pair_re * wave_im + pair_im * wave_re

    def wait_model(p, c):
        o = tile_peer(p)
        model_copy(o, o).wait()
        return c

    lax.fori_loop(1, n_tile, wait_model, 0)
    total = n_tile * chunk
    own_i = iota((4 * R, total), 1)
    sub_col = jnp.concatenate([column([subgrid_ref[k:k + 1, :] for k in range(n_facet)])] * 4, axis=0)
    pick = (sub_col == ((own_i // chunk) * owned + own_i % owned).astype(F32)) & (
        (own_i // owned) % 4 == iota((4 * R, total), 0) // R)
    found = jnp.dot(pick.astype(F32).astype(BF16), model_all[...].reshape(total, quarter),
                    preferred_element_type=F32)
    model_re = jnp.concatenate([found[:R], found[R:2 * R]], axis=1)
    model_im = jnp.concatenate([found[2 * R:3 * R], found[3 * R:]], axis=1)
    image = jnp.concatenate(
        [sre[...] * model_re - sim[...] * model_im, sre[...] * model_im + sim[...] * model_re], axis=0
    ).astype(BF16)

    fr, fc = iota((128, 512), 0), iota((128, 512), 1)
    fold = jnp.where(fr // 32 == fc // 128, fold_values(fr % 32, fc % 128).astype(F32), 0.0).astype(BF16)
    low = iota((R, 128), 1) < 16
    by_x = {}
    for g in range(8):
        got = jnp.dot(image[:, 128 * g:128 * g + 128], fold, preferred_element_type=F32)
        for i in range(4):
            by_x[4 * g + i] = got[:, 128 * i:128 * i + 128]
    for j in range(16):
        up, down = by_x[16 + j], by_x[15 - j]
        even, odd = up + down, up - down
        e_re, e_im, o_re, o_im = even[:R], even[R:], odd[:R], odd[R:]
        parts = (jnp.where(low, e_re, -e_im), -jnp.where(low, o_im, o_re),
                 jnp.where(low, e_im, e_re), jnp.where(low, o_re, -o_im))
        for q in range(4):
            mats[(q * 16 + j) * R:(q * 16 + j + 1) * R, :] = parts[q]

    step = 256

    def table(ref, at, lo):
        return jnp.concatenate([ref[lo // 128 + b, pl.ds(at, 32), :] for b in range(step // 128)], axis=1)

    def degrid(r):
        lhs = mats[pl.ds(r, 64, stride=R), :][:, :32].astype(BF16)
        at = pl.multiple_of(r * 32, 32)
        for lo in range(0, channels, step):
            inner = jnp.dot(lhs, table(tn, at, lo).astype(BF16), preferred_element_type=F32)
            east = table(te, at, lo)
            vre[pl.ds(r, 1), lo:lo + step] = jnp.sum(east * inner[:32], axis=0, keepdims=True)
            vim[pl.ds(r, 1), lo:lo + step] = jnp.sum(east * inner[32:], axis=0, keepdims=True)

    def predict(k, c):
        def group(i, d):
            for n in range(4):
                degrid(k * run + 4 * i + n)
            return d

        lax.fori_loop(0, run // 4, group, 0)
        r0 = pl.multiple_of(k * run, run)
        a_re, a_im = vre[pl.ds(r0, run), :], vim[pl.ds(r0, run), :]
        h_re, h_im = hre[pl.ds(r0, run), :], him[pl.ds(r0, run), :]
        p_re = a_re * h_re + a_im * h_im
        p_im = a_im * h_re - a_re * h_im
        vre[pl.ds(r0, run), :] = p_re
        vim[pl.ds(r0, run), :] = p_im
        pred_send[k, :, :channels] = p_re.astype(BF16)
        pred_send[k, :, channels:] = p_im.astype(BF16)

        def send_pred(p, d):
            pred_copy(facet_peer(p), me_f, k).start()
            return d

        lax.fori_loop(1, n_facet, send_pred, 0)
        return c

    lax.fori_loop(0, n_facet, predict, 0)

    def wait_vis(p, c):
        o = facet_peer(p)
        vis_copy(o, o).wait()
        return c

    lax.fori_loop(1, n_facet, wait_vis, 0)

    def regrid(r):
        at = pl.multiple_of(r * 32, 32)
        acc = jnp.zeros((64, 32), F32)
        for lo in range(0, channels, step):
            east = table(te, at, lo)
            weighted = jnp.concatenate(
                [east * vre[pl.ds(r, 1), lo:lo + step], east * vim[pl.ds(r, 1), lo:lo + step]], axis=0
            ).astype(BF16)
            acc = acc + lax.dot_general(
                weighted, table(tn, at, lo).astype(BF16),
                (((1,), (1,)), ((), ())), preferred_element_type=F32)
        mats[pl.ds(r, 64, stride=R), :] = jnp.concatenate([acc, jnp.zeros((64, 96), F32)], axis=1)

    def grid_block(k, c):
        r0 = pl.multiple_of(k * run, run)

        def wait_pred(p, d):
            o = facet_peer(p)
            pred_copy(o, o, k).wait()
            return d

        lax.fori_loop(1, n_facet, wait_pred, 0)
        res_re = -vre[pl.ds(r0, run), :]
        res_im = -vim[pl.ds(r0, run), :]
        for p in range(1, n_facet):
            other = pred_all[facet_peer(p), k].astype(F32)
            res_re = res_re - other[:, :channels]
            res_im = res_im - other[:, channels:]
        for g in range(n_facet):
            share = (reader_ref[0, k] == g).astype(F32)
            seen = arrived[g].astype(F32) * share
            res_re = res_re + seen[:, :channels]
            res_im = res_im + seen[:, channels:]

        @pl.when(k == me_f)
        def _():
            resid_ref[0, :, :channels] = res_re
            resid_ref[0, :, channels:] = res_im

        h_re, h_im = hre[pl.ds(r0, run), :], him[pl.ds(r0, run), :]
        vre[pl.ds(r0, run), :] = res_re * h_re - res_im * h_im
        vim[pl.ds(r0, run), :] = res_re * h_im + res_im * h_re

        def group(i, d):
            for n in range(4):
                regrid(k * run + 4 * i + n)
            return d

        lax.fori_loop(0, run // 4, group, 0)
        return c

    lax.fori_loop(0, n_facet, grid_block, 0)

    ur, uc = iota((512, 128), 0), iota((512, 128), 1)
    unfold = jnp.where(ur // 128 == uc // 32, fold_values(uc % 32, ur % 128).astype(F32), 0.0).astype(BF16)
    spread = {}
    for j in range(16):
        c_re, s_re, c_im, s_im = (mats[(q * 16 + j) * R:(q * 16 + j + 1) * R, :] for q in range(4))
        for x, sign in ((16 + j, 1.0), (15 - j, -1.0)):
            m = c_re + sign * s_im
            n = c_im - sign * s_re
            spread[x] = jnp.concatenate([jnp.where(low, m, n), jnp.where(low, n, -m)], axis=0).astype(BF16)
    out_re, out_im = [], []
    for g in range(8):
        cells = jnp.dot(jnp.concatenate([spread[4 * g + i] for i in range(4)], axis=1), unfold,
                        preferred_element_type=F32)
        g_re, g_im = cells[:R], cells[R:]
        s_re, s_im = sre[:, 128 * g:128 * g + 128], sim[:, 128 * g:128 * g + 128]
        out_re.append(((s_re * g_re + s_im * g_im) * grid_scale).astype(BF16))
        out_im.append(((s_re * g_im - s_im * g_re) * grid_scale).astype(BF16))
    both = out_re + out_im
    stacked = jnp.concatenate(
        [jnp.concatenate(both[4 * q:4 * q + 4], axis=1) for q in range(4)], axis=0)
    own_r = iota((total, 4 * R), 0)
    sub_row = jnp.sum(
        jnp.where(iota((4 * R, 4 * R), 0) == iota((4 * R, 4 * R), 1), sub_col, 0.0), axis=0, keepdims=True)
    place = (sub_row == ((own_r // chunk) * owned + own_r % owned).astype(F32)) & (
        (own_r // owned) % 4 == iota((total, 4 * R), 1) // R)
    sums = jnp.dot(place.astype(F32).astype(BF16), stacked, preferred_element_type=F32)
    part_send[...] = sums.astype(BF16).reshape(n_tile, chunk, quarter)

    def send_part(p, c):
        part_copy(tile_peer(p), me_t).start()
        return c

    lax.fori_loop(1, n_tile, send_part, 0)

    def add_part(p, acc):
        o = tile_peer(p)
        part_copy(o, o).wait()
        return acc + part_all[o].astype(F32)

    acc = lax.fori_loop(1, n_tile, add_part, part_send[me_t].astype(F32))
    for q in range(4):
        dirty_ref[0, :, q * quarter:(q + 1) * quarter] = acc[q * owned:(q + 1) * owned]


def hand_over(resid_in, dirty_in, resid_out, dirty_out, resid_sem, dirty_sem):
    first = pltpu.make_async_copy(resid_in, resid_out, resid_sem)
    second = pltpu.make_async_copy(dirty_in, dirty_out, dirty_sem)
    first.start()
    second.start()
    first.wait()
    second.wait()


def local(
    sectioned_rows,
    reader,
    baseline_coords,
    subgrid_index,
    stations,
    plane_index,
    model_grid,
    beam_screens,
    plane_phase,
    channel_freq,
):
    n_facet = lax.axis_size("facet")
    n_tile = lax.axis_size("tile")
    channels = channel_freq.shape[0]
    pixels = plane_phase.shape[1]
    run = sectioned_rows.shape[1]
    owned = model_grid.shape[1]
    R = n_facet * run
    chunk, quarter = 4 * owned, 2 * pixels // 4
    grid_scale = 1.0 / math.sqrt(channels * n_facet * (run * n_tile) / (owned * n_tile))

    vmem = pl.BlockSpec(memory_space=pltpu.VMEM)
    body = functools.partial(kernel, n_facet, n_tile, owned, run, channels, grid_scale)
    dma = pltpu.SemaphoreType.DMA
    resid, dirty = pl.pallas_call(
        body,
        out_shape=(
            jax.ShapeDtypeStruct((1, run, 2 * channels), F32),
            jax.ShapeDtypeStruct((1, owned, 2 * pixels), F32),
        ),
        in_specs=[pl.BlockSpec(memory_space=pltpu.SMEM)] + [vmem] * 6
        + [pl.BlockSpec(memory_space=pl.ANY)] + [vmem] * 2,
        out_specs=(vmem, vmem),
        scratch_shapes=[
            pltpu.VMEM((R, 2), F32),
            pltpu.VMEM(beam_screens.shape[1:], BF16),
            pltpu.VMEM((chunk, quarter), BF16),
            pltpu.VMEM((n_tile, chunk, quarter), BF16),
            pltpu.VMEM((n_facet, run, 2 * channels), BF16),
            pltpu.VMEM((n_facet, run, 2 * channels), BF16),
            pltpu.VMEM((n_facet, n_facet, run, 2 * channels), BF16),
            pltpu.VMEM((n_tile, chunk, quarter), BF16),
            pltpu.VMEM((n_tile, chunk, quarter), BF16),
            pltpu.VMEM((channels // 128, R * 32, 128), F32),
            pltpu.VMEM((channels // 128, R * 32, 128), F32),
            pltpu.VMEM((64 * R, 128), F32),
            pltpu.VMEM((R, channels), F32),
            pltpu.VMEM((R, channels), F32),
            pltpu.VMEM((R, channels), F32),
            pltpu.VMEM((R, channels), F32),
            pltpu.VMEM((R, pixels), F32),
            pltpu.VMEM((R, pixels), F32),
            dma,
            dma((n_tile,)), dma((n_tile,)),
            dma((n_facet,)), dma((n_facet,)),
            dma((n_facet, n_facet)), dma((n_facet, n_facet)),
            dma((n_tile,)), dma((n_tile,)),
        ],
        compiler_params=pltpu.CompilerParams(
            collective_id=0, has_side_effects=True, vmem_limit_bytes=60 * 1024 * 1024),
        name="predict_regrid",
    )(reader, baseline_coords, subgrid_index, stations, plane_index, sectioned_rows, model_grid,
      beam_screens[0], plane_phase, channel_freq[None, :])
    anywhere = pl.BlockSpec(memory_space=pl.ANY)
    return pl.pallas_call(
        hand_over,
        out_shape=(
            jax.ShapeDtypeStruct(resid.shape, F32),
            jax.ShapeDtypeStruct(dirty.shape, F32),
        ),
        in_specs=[anywhere] * 2,
        out_specs=(anywhere, anywhere),
        scratch_shapes=[dma, dma],
        name="hand_over",
    )(resid, dirty)


def solution(mesh):
    return jax.shard_map(
        local,
        mesh=mesh,
        in_specs=(
            P("facet", "tile", None),
            P("tile", None),
            P(None, None, "tile"),
            P(None, "tile"),
            P(None, None, "tile"),
            P(None, "tile"),
            P("facet", "tile", None),
            P("facet", None, None),
            P(),
            P(),
        ),
        out_specs=(P("facet", "tile", None), P("facet", "tile", None)),
        check_vma=False,
    )
```

```python
import functools
import math

import jax
import jax.numpy as jnp
from jax import lax
from jax.experimental import pallas as pl
from jax.experimental.pallas import tpu as pltpu
from jax.sharding import PartitionSpec as P

MESH = pl.DeviceIdType.MESH
F32 = jnp.float32
BF16 = jnp.bfloat16


def cos_sin(x):
    y = x * x
    c = 1.0 / math.factorial(12)
    s = 1.0 / math.factorial(13)
    for k in range(5, -1, -1):
        sign = -1.0 if k % 2 else 1.0
        c = c * y + sign / math.factorial(2 * k)
        s = s * y + sign / math.factorial(2 * k + 1)
    return c, s * x


def iota(shape, dim):
    return lax.broadcasted_iota(jnp.int32, shape, dim)


def fold_values(cell, part_col):
    k = part_col % 16
    odd = part_col // 16
    hit = (cell == 16 + k).astype(F32)
    other = (cell == 15 - k).astype(F32)
    value = hit + other * (1.0 - 2.0 * odd.astype(F32))
    return jnp.where(part_col < 32, value, 0.0).astype(BF16)


def column(rows):
    n = rows[0].shape[1]
    diagonal = iota((n, n), 0) == iota((n, n), 1)
    return jnp.concatenate(
        [jnp.sum(jnp.where(diagonal, row.astype(F32), 0.0), axis=1, keepdims=True) for row in rows], axis=0)


def kernel(
    n_facet, n_tile, owned, run, channels, grid_scale,
    reader_ref, coords_ref, subgrid_ref, stations_ref, plane_ref, rows_ref, model_ref, screens_hbm, phase_ref, freq_ref,
    resid_ref, dirty_ref,
    cols, screens, model_send, model_all, arrived, pred_send, pred_all, part_send, part_all,
    te, tn, mats, hre, him, vre, vim, sre, sim,
    local_sem, model_ss, model_rs, vis_ss, vis_rs, pred_ss, pred_rs, part_ss, part_rs,
):
    R = n_facet * run
    me_f = lax.axis_index("facet")
    me_t = lax.axis_index("tile")
    chunk = model_send.shape[0]
    quarter = model_send.shape[1]

    load = pltpu.make_async_copy(screens_hbm, screens, local_sem)
    load.start()

    def tile_peer(p):
        return lax.rem(me_t + p, n_tile)

    def facet_peer(p):
        return lax.rem(me_f + p, n_facet)

    barrier = pltpu.get_barrier_semaphore()

    def greet_tile(p, c):
        pl.semaphore_signal(barrier, inc=1, device_id=(me_f, tile_peer(p)), device_id_type=MESH)
        return c

    def greet_facet(p, c):
        pl.semaphore_signal(barrier, inc=1, device_id=(facet_peer(p), me_t), device_id_type=MESH)
        return c

    lax.fori_loop(1, n_tile, greet_tile, 0)
    lax.fori_loop(1, n_facet, greet_facet, 0)

    model_f = model_ref[0].astype(F32)
    model_send[...] = jnp.concatenate(
        [model_f[:, q * quarter:(q + 1) * quarter] for q in range(4)], axis=0
    ).astype(BF16)
    for axis in range(2):
        cols[:, axis:axis + 1] = column([coords_ref[k, axis:axis + 1, :] for k in range(n_facet)])

    pr, pc = iota((256, 256), 0), iota((256, 256), 1)
    perm = ((pr // 32 == pc % 8) & (pr % 32 == pc // 8)).astype(F32).astype(BF16)
    perm_back = ((pr // 8 == pc % 32) & (pr % 8 == pc // 32)).astype(F32).astype(BF16)
    step = 256

    def tables(axis, dst):
        def group(g, c):
            r0 = pl.multiple_of(g * 8, 8)
            at = pl.multiple_of(g * 256, 256)
            u = cols[pl.ds(r0, 8), axis:axis + 1] * (2.0 * math.pi / 64.0)
            for lo in range(0, channels, step):
                lanes = slice(lo, lo + step)
                c0, s0 = cos_sin(u * freq_ref[:, lanes])
                twice = 2.0 - 4.0 * s0 * s0
                cos_rows, sin_rows = [c0, twice * c0 - c0], [s0, twice * s0 + s0]
                for j in range(2, 16):
                    cos_rows.append(twice * cos_rows[-1] - cos_rows[-2])
                    sin_rows.append(twice * sin_rows[-1] - sin_rows[-2])
                rows = jnp.concatenate(cos_rows + sin_rows, axis=0).astype(BF16)
                moved = jnp.dot(perm, rows, preferred_element_type=F32)
                dst[pl.ds(at, 256), lanes] = moved.astype(dst.dtype)
                if axis == 0:
                    hre[pl.ds(r0, 8), lanes] = c0
                    him[pl.ds(r0, 8), lanes] = s0
                else:
                    ca, sa = hre[pl.ds(r0, 8), lanes], him[pl.ds(r0, 8), lanes]
                    hre[pl.ds(r0, 8), lanes] = ca * c0 - sa * s0
                    him[pl.ds(r0, 8), lanes] = ca * s0 + sa * c0
            return c

        lax.fori_loop(0, R // 8, group, 0)

    tables(0, te)
    pl.semaphore_wait(barrier, n_tile + n_facet - 2)

    def model_copy(o, slot):
        return pltpu.make_async_remote_copy(
            src_ref=model_send, dst_ref=model_all.at[slot], send_sem=model_ss.at[o],
            recv_sem=model_rs.at[slot], device_id=(me_f, o), device_id_type=MESH)

    def vis_copy(o, slot):
        return pltpu.make_async_remote_copy(
            src_ref=rows_ref.at[0], dst_ref=arrived.at[slot], send_sem=vis_ss.at[o],
            recv_sem=vis_rs.at[slot], device_id=(o, me_t), device_id_type=MESH)

    def pred_copy(o, slot, k):
        return pltpu.make_async_remote_copy(
            src_ref=pred_send.at[k], dst_ref=pred_all.at[slot, k], send_sem=pred_ss.at[o, k],
            recv_sem=pred_rs.at[slot, k], device_id=(o, me_t), device_id_type=MESH)

    def part_copy(o, slot):
        return pltpu.make_async_remote_copy(
            src_ref=part_send.at[o], dst_ref=part_all.at[slot], send_sem=part_ss.at[o],
            recv_sem=part_rs.at[slot], device_id=(me_f, o), device_id_type=MESH)

    def send_model(p, c):
        model_copy(tile_peer(p), me_t).start()
        return c

    def send_vis(p, c):
        vis_copy(facet_peer(p), me_f).start()
        return c

    lax.fori_loop(1, n_tile, send_model, 0)
    lax.fori_loop(1, n_facet, send_vis, 0)
    model_all[me_t] = model_send[...]
    arrived[me_f] = rows_ref[0]

    tables(1, tn)

    stations = screens.shape[0]
    planes, pixels = phase_ref.shape
    half_c, half_s = cos_sin(phase_ref[...] * 0.5)
    waves = jnp.concatenate([1.0 - 2.0 * half_s * half_s, 2.0 * half_s * half_c], axis=1)
    plane_hot = (column([plane_ref[k:k + 1, :] for k in range(n_facet)]) == iota((R, planes), 1).astype(F32)).astype(F32)
    wave = jnp.dot(plane_hot, waves, preferred_element_type=F32, precision=lax.Precision.HIGHEST)
    wave_re, wave_im = wave[:, :pixels], wave[:, pixels:]
    load.wait()
    pair_col = column([stations_ref[k, a:a + 1, :] for a in range(2) for k in range(n_facet)])
    station_hot = (pair_col == iota((2 * R, stations), 1).astype(F32)).astype(F32).astype(BF16)
    both_rows = jnp.dot(station_hot, screens[...], preferred_element_type=F32)
    one, two = both_rows[:R], both_rows[R:]
    one_re, one_im, two_re, two_im = one[:, :pixels], one[:, pixels:], two[:, :pixels], two[:, pixels:]
    pair_re = one_re * two_re + one_im * two_im
    pair_im = one_im * two_re - one_re * two_im
    sre[...] = pair_re * wave_re - pair_im * wave_im
    sim[...] = pair_re * wave_im + pair_im * wave_re

    def wait_model(p, c):
        o = tile_peer(p)
        model_copy(o, o).wait()
        return c

    lax.fori_loop(1, n_tile, wait_model, 0)
    total = n_tile * chunk
    own_i = iota((4 * R, total), 1)
    sub_col = jnp.concatenate([column([subgrid_ref[k:k + 1, :] for k in range(n_facet)])] * 4, axis=0)
    pick = (sub_col == ((own_i // chunk) * owned + own_i % owned).astype(F32)) & (
        (own_i // owned) % 4 == iota((4 * R, total), 0) // R)
    found = jnp.dot(pick.astype(F32).astype(BF16), model_all[...].reshape(total, quarter),
                    preferred_element_type=F32)
    model_re = jnp.concatenate([found[:R], found[R:2 * R]], axis=1)
    model_im = jnp.concatenate([found[2 * R:3 * R], found[3 * R:]], axis=1)
    image = jnp.concatenate(
        [sre[...] * model_re - sim[...] * model_im, sre[...] * model_im + sim[...] * model_re], axis=0
    ).astype(BF16)

    fr, fc = iota((128, 512), 0), iota((128, 512), 1)
    fold = jnp.where(fr // 32 == fc // 128, fold_values(fr % 32, fc % 128).astype(F32), 0.0).astype(BF16)
    low = iota((R, 128), 1) < 16
    by_x, folded = {}, {}
    for g in range(8):
        got = jnp.dot(image[:, 128 * g:128 * g + 128], fold, preferred_element_type=F32)
        for i in range(4):
            by_x[4 * g + i] = got[:, 128 * i:128 * i + 128]
    for j in range(16):
        up, down = by_x[16 + j], by_x[15 - j]
        even, odd = up + down, up - down
        e_re, e_im, o_re, o_im = even[:R], even[R:], odd[:R], odd[R:]
        parts = (jnp.where(low, e_re, -e_im), -jnp.where(low, o_im, o_re),
                 jnp.where(low, e_im, e_re), jnp.where(low, o_re, -o_im))
        for q in range(4):
            folded[q * 16 + j] = parts[q].astype(BF16)
    for lot in range(8):
        for r0 in range(0, R, 32):
            cells = jnp.concatenate([folded[8 * lot + m][r0:r0 + 32] for m in range(8)], axis=0)
            moved = jnp.dot(perm_back, cells, preferred_element_type=F32)
            mats[r0:r0 + 32, 8 * lot:8 * lot + 8, :] = moved.reshape(32, 8, 128)

    def degrid(r):
        lhs = mats[r][:, :32].astype(BF16)
        at = pl.multiple_of(r * 32, 32)
        for lo in range(0, channels, step):
            inner = jnp.dot(lhs, tn[pl.ds(at, 32), lo:lo + step], preferred_element_type=F32)
            east = te[pl.ds(at, 32), lo:lo + step]
            vre[pl.ds(r, 1), lo:lo + step] = jnp.sum(east * inner[:32], axis=0, keepdims=True)
            vim[pl.ds(r, 1), lo:lo + step] = jnp.sum(east * inner[32:], axis=0, keepdims=True)

    def predict(k, c):
        def group(i, d):
            for n in range(4):
                degrid(k * run + 4 * i + n)
            return d

        lax.fori_loop(0, run // 4, group, 0)
        r0 = pl.multiple_of(k * run, run)
        a_re, a_im = vre[pl.ds(r0, run), :], vim[pl.ds(r0, run), :]
        h_re, h_im = hre[pl.ds(r0, run), :], him[pl.ds(r0, run), :]
        p_re = a_re * h_re + a_im * h_im
        p_im = a_im * h_re - a_re * h_im
        vre[pl.ds(r0, run), :] = p_re
        vim[pl.ds(r0, run), :] = p_im
        pred_send[k, :, :channels] = p_re.astype(BF16)
        pred_send[k, :, channels:] = p_im.astype(BF16)

        def send_pred(p, d):
            pred_copy(facet_peer(p), me_f, k).start()
            return d

        lax.fori_loop(1, n_facet, send_pred, 0)
        return c

    lax.fori_loop(0, n_facet, predict, 0)

    def wait_vis(p, c):
        o = facet_peer(p)
        vis_copy(o, o).wait()
        return c

    lax.fori_loop(1, n_facet, wait_vis, 0)

    def regrid(r):
        at = pl.multiple_of(r * 32, 32)
        acc = jnp.zeros((64, 32), F32)
        for lo in range(0, channels, step):
            east = te[pl.ds(at, 32), lo:lo + step]
            weighted = jnp.concatenate(
                [east * vre[pl.ds(r, 1), lo:lo + step], east * vim[pl.ds(r, 1), lo:lo + step]], axis=0
            ).astype(BF16)
            acc = acc + lax.dot_general(
                weighted, tn[pl.ds(at, 32), lo:lo + step],
                (((1,), (1,)), ((), ())), preferred_element_type=F32)
        cos_lane = iota((16, 32), 1) < 16
        c_re, s_re, c_im, s_im = (acc[16 * q:16 * q + 16] for q in range(4))
        m_up, m_down, n_up, n_down = c_re + s_im, c_re - s_im, c_im - s_re, c_im + s_re
        cells = jnp.concatenate(
            [jnp.where(cos_lane, m_up, n_up), jnp.where(cos_lane, m_down, n_down),
             jnp.where(cos_lane, n_up, -m_up), jnp.where(cos_lane, n_down, -m_down)], axis=0)
        mats[r] = jnp.concatenate([cells, jnp.zeros((64, 96), F32)], axis=1)

    def grid_block(k, c):
        r0 = pl.multiple_of(k * run, run)

        def wait_pred(p, d):
            o = facet_peer(p)
            pred_copy(o, o, k).wait()
            return d

        lax.fori_loop(1, n_facet, wait_pred, 0)
        res_re = -vre[pl.ds(r0, run), :]
        res_im = -vim[pl.ds(r0, run), :]
        for p in range(1, n_facet):
            other = pred_all[facet_peer(p), k].astype(F32)
            res_re = res_re - other[:, :channels]
            res_im = res_im - other[:, channels:]
        for g in range(n_facet):
            share = (reader_ref[0, k] == g).astype(F32)
            seen = arrived[g].astype(F32) * share
            res_re = res_re + seen[:, :channels]
            res_im = res_im + seen[:, channels:]

        @pl.when(k == me_f)
        def _():
            resid_ref[0, :, :channels] = res_re
            resid_ref[0, :, channels:] = res_im

        h_re, h_im = hre[pl.ds(r0, run), :], him[pl.ds(r0, run), :]
        vre[pl.ds(r0, run), :] = res_re * h_re - res_im * h_im
        vim[pl.ds(r0, run), :] = res_re * h_im + res_im * h_re

        def group(i, d):
            for n in range(4):
                regrid(k * run + 4 * i + n)
            return d

        lax.fori_loop(0, run // 4, group, 0)
        return c

    lax.fori_loop(0, n_facet, grid_block, 0)

    ur, uc = iota((512, 128), 0), iota((512, 128), 1)
    unfold = jnp.where(ur // 128 == uc // 32, fold_values(uc % 32, ur % 128).astype(F32), 0.0).astype(BF16)
    spread = {}
    for lot in range(8):
        moved = [jnp.dot(perm, mats[r0:r0 + 32, 8 * lot:8 * lot + 8, :].reshape(256, 128).astype(BF16),
                         preferred_element_type=F32).astype(BF16) for r0 in range(0, R, 32)]
        for m in range(8):
            part, place_x = divmod(8 * lot + m, 32)
            x = 16 + place_x if place_x < 16 else 31 - place_x
            spread[part, x] = [got[32 * m:32 * m + 32] for got in moved]
    spread = {x: jnp.concatenate(spread[0, x] + spread[1, x], axis=0) for x in range(32)}
    out_re, out_im = [], []
    for g in range(8):
        cells = jnp.dot(jnp.concatenate([spread[4 * g + i] for i in range(4)], axis=1), unfold,
                        preferred_element_type=F32)
        g_re, g_im = cells[:R], cells[R:]
        s_re, s_im = sre[:, 128 * g:128 * g + 128], sim[:, 128 * g:128 * g + 128]
        out_re.append(((s_re * g_re + s_im * g_im) * grid_scale).astype(BF16))
        out_im.append(((s_re * g_im - s_im * g_re) * grid_scale).astype(BF16))
    both = out_re + out_im
    stacked = jnp.concatenate(
        [jnp.concatenate(both[4 * q:4 * q + 4], axis=1) for q in range(4)], axis=0)
    own_r = iota((total, 4 * R), 0)
    sub_row = jnp.sum(
        jnp.where(iota((4 * R, 4 * R), 0) == iota((4 * R, 4 * R), 1), sub_col, 0.0), axis=0, keepdims=True)
    place = (sub_row == ((own_r // chunk) * owned + own_r % owned).astype(F32)) & (
        (own_r // owned) % 4 == iota((total, 4 * R), 1) // R)
    sums = jnp.dot(place.astype(F32).astype(BF16), stacked, preferred_element_type=F32)
    part_send[...] = sums.astype(BF16).reshape(n_tile, chunk, quarter)

    def send_part(p, c):
        part_copy(tile_peer(p), me_t).start()
        return c

    lax.fori_loop(1, n_tile, send_part, 0)

    def add_part(p, acc):
        o = tile_peer(p)
        part_copy(o, o).wait()
        return acc + part_all[o].astype(F32)

    acc = lax.fori_loop(1, n_tile, add_part, part_send[me_t].astype(F32))
    for q in range(4):
        dirty_ref[0, :, q * quarter:(q + 1) * quarter] = acc[q * owned:(q + 1) * owned]


def hand_over(resid_in, dirty_in, resid_out, dirty_out):
    resid_out[...] = resid_in[...]
    dirty_out[...] = dirty_in[...]


def local(
    sectioned_rows,
    reader,
    baseline_coords,
    subgrid_index,
    stations,
    plane_index,
    model_grid,
    beam_screens,
    plane_phase,
    channel_freq,
):
    n_facet = lax.axis_size("facet")
    n_tile = lax.axis_size("tile")
    channels = channel_freq.shape[0]
    pixels = plane_phase.shape[1]
    run = sectioned_rows.shape[1]
    owned = model_grid.shape[1]
    R = n_facet * run
    chunk, quarter = 4 * owned, 2 * pixels // 4
    grid_scale = 1.0 / math.sqrt(channels * n_facet * (run * n_tile) / (owned * n_tile))

    vmem = pl.BlockSpec(memory_space=pltpu.VMEM)
    body = functools.partial(kernel, n_facet, n_tile, owned, run, channels, grid_scale)
    dma = pltpu.SemaphoreType.DMA
    resid, dirty = pl.pallas_call(
        body,
        out_shape=(
            jax.ShapeDtypeStruct((1, run, 2 * channels), F32),
            jax.ShapeDtypeStruct((1, owned, 2 * pixels), F32),
        ),
        in_specs=[pl.BlockSpec(memory_space=pltpu.SMEM)] + [vmem] * 6
        + [pl.BlockSpec(memory_space=pl.ANY)] + [vmem] * 2,
        out_specs=(vmem, vmem),
        scratch_shapes=[
            pltpu.VMEM((R, 2), F32),
            pltpu.VMEM(beam_screens.shape[1:], BF16),
            pltpu.VMEM((chunk, quarter), BF16),
            pltpu.VMEM((n_tile, chunk, quarter), BF16),
            pltpu.VMEM((n_facet, run, 2 * channels), BF16),
            pltpu.VMEM((n_facet, run, 2 * channels), BF16),
            pltpu.VMEM((n_facet, n_facet, run, 2 * channels), BF16),
            pltpu.VMEM((n_tile, chunk, quarter), BF16),
            pltpu.VMEM((n_tile, chunk, quarter), BF16),
            pltpu.VMEM((R * 32, channels), F32),
            pltpu.VMEM((R * 32, channels), BF16),
            pltpu.VMEM((R, 64, 128), F32),
            pltpu.VMEM((R, channels), F32),
            pltpu.VMEM((R, channels), F32),
            pltpu.VMEM((R, channels), F32),
            pltpu.VMEM((R, channels), F32),
            pltpu.VMEM((R, pixels), F32),
            pltpu.VMEM((R, pixels), F32),
            dma,
            dma((n_tile,)), dma((n_tile,)),
            dma((n_facet,)), dma((n_facet,)),
            dma((n_facet, n_facet)), dma((n_facet, n_facet)),
            dma((n_tile,)), dma((n_tile,)),
        ],
        compiler_params=pltpu.CompilerParams(
            collective_id=0, has_side_effects=True, vmem_limit_bytes=60 * 1024 * 1024),
        name="predict_regrid",
    )(reader, baseline_coords, subgrid_index, stations, plane_index, sectioned_rows, model_grid,
      beam_screens[0], plane_phase, channel_freq[None, :])
    return pl.pallas_call(
        hand_over,
        out_shape=(
            jax.ShapeDtypeStruct(resid.shape, F32),
            jax.ShapeDtypeStruct(dirty.shape, F32),
        ),
        in_specs=[vmem] * 2,
        out_specs=(vmem, vmem),
        name="hand_over",
    )(resid, dirty)


def solution(mesh):
    return jax.shard_map(
        local,
        mesh=mesh,
        in_specs=(
            P("facet", "tile", None),
            P("tile", None),
            P(None, None, "tile"),
            P(None, "tile"),
            P(None, None, "tile"),
            P(None, "tile"),
            P("facet", "tile", None),
            P("facet", None, None),
            P(),
            P(),
        ),
        out_specs=(P("facet", "tile", None), P("facet", "tile", None)),
        check_vma=False,
    )
```

```python
import functools
import math

import jax
import jax.numpy as jnp
from jax import lax
from jax.experimental import pallas as pl
from jax.experimental.pallas import tpu as pltpu
from jax.sharding import PartitionSpec as P

MESH = pl.DeviceIdType.MESH
F32 = jnp.float32
BF16 = jnp.bfloat16


def cos_sin(x):
    y = x * x
    c = 1.0 / math.factorial(12)
    s = 1.0 / math.factorial(13)
    for k in range(5, -1, -1):
        sign = -1.0 if k % 2 else 1.0
        c = c * y + sign / math.factorial(2 * k)
        s = s * y + sign / math.factorial(2 * k + 1)
    return c, s * x


def iota(shape, dim):
    return lax.broadcasted_iota(jnp.int32, shape, dim)


def fold_values(cell, part_col):
    k = part_col % 16
    odd = part_col // 16
    hit = (cell == 16 + k).astype(F32)
    other = (cell == 15 - k).astype(F32)
    value = hit + other * (1.0 - 2.0 * odd.astype(F32))
    return jnp.where(part_col < 32, value, 0.0).astype(BF16)


def column(rows):
    n = rows[0].shape[1]
    diagonal = iota((n, n), 0) == iota((n, n), 1)
    return jnp.concatenate(
        [jnp.sum(jnp.where(diagonal, row.astype(F32), 0.0), axis=1, keepdims=True) for row in rows], axis=0)


def kernel(
    n_facet, n_tile, owned, run, channels, grid_scale,
    reader_ref, coords_ref, subgrid_ref, stations_ref, plane_ref, rows_ref, model_ref, screens_hbm, phase_ref, freq_ref,
    resid_ref, dirty_ref,
    cols, screens, model_send, model_all, arrived, pred_send, pred_all, part_send, part_all,
    te, tn, mats, weighted, hre, him, vre, vim, sre, sim,
    local_sem, model_ss, model_rs, vis_ss, vis_rs, pred_ss, pred_rs, part_ss, part_rs,
):
    R = n_facet * run
    me_f = lax.axis_index("facet")
    me_t = lax.axis_index("tile")
    chunk = model_send.shape[0]
    quarter = model_send.shape[1]

    load = pltpu.make_async_copy(screens_hbm, screens, local_sem)
    load.start()

    def tile_peer(p):
        return lax.rem(me_t + p, n_tile)

    def facet_peer(p):
        return lax.rem(me_f + p, n_facet)

    barrier = pltpu.get_barrier_semaphore()

    def greet_tile(p, c):
        pl.semaphore_signal(barrier, inc=1, device_id=(me_f, tile_peer(p)), device_id_type=MESH)
        return c

    def greet_facet(p, c):
        pl.semaphore_signal(barrier, inc=1, device_id=(facet_peer(p), me_t), device_id_type=MESH)
        return c

    lax.fori_loop(1, n_tile, greet_tile, 0)
    lax.fori_loop(1, n_facet, greet_facet, 0)

    model_f = model_ref[0].astype(F32)
    model_send[...] = jnp.concatenate(
        [model_f[:, q * quarter:(q + 1) * quarter] for q in range(4)], axis=0
    ).astype(BF16)
    for axis in range(2):
        cols[:, axis:axis + 1] = column([coords_ref[k, axis:axis + 1, :] for k in range(n_facet)])

    pr, pc = iota((256, 256), 0), iota((256, 256), 1)
    perm = ((pr // 32 == pc % 8) & (pr % 32 == pc // 8)).astype(F32).astype(BF16)
    perm_back = ((pr // 8 == pc % 32) & (pr % 8 == pc // 32)).astype(F32).astype(BF16)
    step = 256

    def tables(axis, dst):
        def group(g, c):
            r0 = pl.multiple_of(g * 8, 8)
            at = pl.multiple_of(g * 256, 256)
            u = cols[pl.ds(r0, 8), axis:axis + 1] * (2.0 * math.pi / 64.0)
            for lo in range(0, channels, step):
                lanes = slice(lo, lo + step)
                c0, s0 = cos_sin(u * freq_ref[:, lanes])
                twice = 2.0 - 4.0 * s0 * s0
                cos_rows, sin_rows = [c0, twice * c0 - c0], [s0, twice * s0 + s0]
                for j in range(2, 16):
                    cos_rows.append(twice * cos_rows[-1] - cos_rows[-2])
                    sin_rows.append(twice * sin_rows[-1] - sin_rows[-2])
                rows = jnp.concatenate(cos_rows + sin_rows, axis=0).astype(BF16)
                moved = jnp.dot(perm, rows, preferred_element_type=F32)
                dst[pl.ds(at, 256), lanes] = moved.astype(dst.dtype)
                if axis == 0:
                    hre[pl.ds(r0, 8), lanes] = c0
                    him[pl.ds(r0, 8), lanes] = s0
                else:
                    ca, sa = hre[pl.ds(r0, 8), lanes], him[pl.ds(r0, 8), lanes]
                    hre[pl.ds(r0, 8), lanes] = ca * c0 - sa * s0
                    him[pl.ds(r0, 8), lanes] = ca * s0 + sa * c0
            return c

        lax.fori_loop(0, R // 8, group, 0)

    tables(0, te)
    pl.semaphore_wait(barrier, n_tile + n_facet - 2)

    def model_copy(o, slot):
        return pltpu.make_async_remote_copy(
            src_ref=model_send, dst_ref=model_all.at[slot], send_sem=model_ss.at[o],
            recv_sem=model_rs.at[slot], device_id=(me_f, o), device_id_type=MESH)

    def vis_copy(o, slot):
        return pltpu.make_async_remote_copy(
            src_ref=rows_ref.at[0], dst_ref=arrived.at[slot], send_sem=vis_ss.at[o],
            recv_sem=vis_rs.at[slot], device_id=(o, me_t), device_id_type=MESH)

    def pred_copy(o, slot, k):
        return pltpu.make_async_remote_copy(
            src_ref=pred_send.at[k], dst_ref=pred_all.at[slot, k], send_sem=pred_ss.at[o, k],
            recv_sem=pred_rs.at[slot, k], device_id=(o, me_t), device_id_type=MESH)

    def part_copy(o, slot):
        return pltpu.make_async_remote_copy(
            src_ref=part_send.at[o], dst_ref=part_all.at[slot], send_sem=part_ss.at[o],
            recv_sem=part_rs.at[slot], device_id=(me_f, o), device_id_type=MESH)

    def send_model(p, c):
        model_copy(tile_peer(p), me_t).start()
        return c

    def send_vis(p, c):
        vis_copy(facet_peer(p), me_f).start()
        return c

    lax.fori_loop(1, n_tile, send_model, 0)
    lax.fori_loop(1, n_facet, send_vis, 0)
    model_all[me_t] = model_send[...]
    arrived[me_f] = rows_ref[0]

    tables(1, tn)

    stations = screens.shape[0]
    planes, pixels = phase_ref.shape
    half_c, half_s = cos_sin(phase_ref[...] * 0.5)
    waves = jnp.concatenate([1.0 - 2.0 * half_s * half_s, 2.0 * half_s * half_c], axis=1)
    plane_hot = (column([plane_ref[k:k + 1, :] for k in range(n_facet)]) == iota((R, planes), 1).astype(F32)).astype(F32)
    wave = jnp.dot(plane_hot, waves, preferred_element_type=F32, precision=lax.Precision.HIGHEST)
    wave_re, wave_im = wave[:, :pixels], wave[:, pixels:]
    load.wait()
    pair_col = column([stations_ref[k, a:a + 1, :] for a in range(2) for k in range(n_facet)])
    station_hot = (pair_col == iota((2 * R, stations), 1).astype(F32)).astype(F32).astype(BF16)
    both_rows = jnp.dot(station_hot, screens[...], preferred_element_type=F32)
    one, two = both_rows[:R], both_rows[R:]
    one_re, one_im, two_re, two_im = one[:, :pixels], one[:, pixels:], two[:, :pixels], two[:, pixels:]
    pair_re = one_re * two_re + one_im * two_im
    pair_im = one_im * two_re - one_re * two_im
    sre[...] = pair_re * wave_re - pair_im * wave_im
    sim[...] = pair_re * wave_im + pair_im * wave_re

    def wait_model(p, c):
        o = tile_peer(p)
        model_copy(o, o).wait()
        return c

    lax.fori_loop(1, n_tile, wait_model, 0)
    total = n_tile * chunk
    own_i = iota((4 * R, total), 1)
    sub_col = jnp.concatenate([column([subgrid_ref[k:k + 1, :] for k in range(n_facet)])] * 4, axis=0)
    pick = (sub_col == ((own_i // chunk) * owned + own_i % owned).astype(F32)) & (
        (own_i // owned) % 4 == iota((4 * R, total), 0) // R)
    found = jnp.dot(pick.astype(F32).astype(BF16), model_all[...].reshape(total, quarter),
                    preferred_element_type=F32)
    model_re = jnp.concatenate([found[:R], found[R:2 * R]], axis=1)
    model_im = jnp.concatenate([found[2 * R:3 * R], found[3 * R:]], axis=1)
    image = jnp.concatenate(
        [sre[...] * model_re - sim[...] * model_im, sre[...] * model_im + sim[...] * model_re], axis=0
    ).astype(BF16)

    fr, fc = iota((128, 1024), 0), iota((128, 1024), 1)
    fold = jnp.where(fr // 32 == fc // 256, fold_values(fr % 32, fc % 32).astype(F32), 0.0).astype(BF16)
    low = iota((R, 256), 1) % 32 < 16
    diagonal = pr // 8 % 8 == pc // 32
    by_x, folded = {}, {}
    for g in range(8):
        got = jnp.dot(image[:, 128 * g:128 * g + 128], fold, preferred_element_type=F32)
        for i in range(4):
            by_x[4 * g + i] = got[:, 256 * i:256 * i + 256]
    for j in range(16):
        up, down = by_x[16 + j], by_x[15 - j]
        even, odd = up + down, up - down
        e_re, e_im, o_re, o_im = even[:R], even[R:], odd[:R], odd[R:]
        parts = (jnp.where(low, e_re, -e_im), -jnp.where(low, o_im, o_re),
                 jnp.where(low, e_im, e_re), jnp.where(low, o_re, -o_im))
        for q in range(4):
            folded[q * 16 + j] = parts[q].astype(BF16)
    for lot in range(8):
        for r0 in range(0, R, 32):
            cells = jnp.concatenate([folded[8 * lot + m][r0:r0 + 32] for m in range(8)], axis=0)
            moved = jnp.dot(perm_back, cells, preferred_element_type=F32)
            mats[r0:r0 + 32, 8 * lot:8 * lot + 8, :] = jnp.where(diagonal, moved, 0.0).reshape(32, 8, 256)

    def degrid(g):
        r0 = pl.multiple_of(g * 8, 8)
        at = pl.multiple_of(g * 256, 256)
        lhs = mats[pl.ds(r0, 8)].reshape(512, 256).astype(BF16)
        for lo in range(0, channels, step):
            inner = jnp.dot(lhs, tn[pl.ds(at, 256), lo:lo + step], preferred_element_type=F32)
            for n in range(8):
                east = te[pl.ds(at + 32 * n, 32), lo:lo + step]
                vre[pl.ds(r0 + n, 1), lo:lo + step] = jnp.sum(
                    east * inner[64 * n:64 * n + 32], axis=0, keepdims=True)
                vim[pl.ds(r0 + n, 1), lo:lo + step] = jnp.sum(
                    east * inner[64 * n + 32:64 * n + 64], axis=0, keepdims=True)

    def predict(k, c):
        def group(i, d):
            degrid(k * (run // 8) + i)
            return d

        lax.fori_loop(0, run // 8, group, 0)
        r0 = pl.multiple_of(k * run, run)
        a_re, a_im = vre[pl.ds(r0, run), :], vim[pl.ds(r0, run), :]
        h_re, h_im = hre[pl.ds(r0, run), :], him[pl.ds(r0, run), :]
        p_re = a_re * h_re + a_im * h_im
        p_im = a_im * h_re - a_re * h_im
        vre[pl.ds(r0, run), :] = p_re
        vim[pl.ds(r0, run), :] = p_im
        pred_send[k, :, :channels] = p_re.astype(BF16)
        pred_send[k, :, channels:] = p_im.astype(BF16)

        def send_pred(p, d):
            pred_copy(facet_peer(p), me_f, k).start()
            return d

        lax.fori_loop(1, n_facet, send_pred, 0)
        return c

    lax.fori_loop(0, n_facet, predict, 0)

    def wait_vis(p, c):
        o = facet_peer(p)
        vis_copy(o, o).wait()
        return c

    lax.fori_loop(1, n_facet, wait_vis, 0)

    def regrid(g):
        r0 = pl.multiple_of(g * 8, 8)
        at = pl.multiple_of(g * 256, 256)
        for n in range(8):
            for lo in range(0, channels, step):
                east = te[pl.ds(at + 32 * n, 32), lo:lo + step]
                weighted[64 * n:64 * n + 32, lo:lo + step] = (east * vre[pl.ds(r0 + n, 1), lo:lo + step]).astype(BF16)
                weighted[64 * n + 32:64 * n + 64, lo:lo + step] = (east * vim[pl.ds(r0 + n, 1), lo:lo + step]).astype(BF16)
        acc = lax.dot_general(weighted[...], tn[pl.ds(at, 256), :], (((1,), (1,)), ((), ())),
                              preferred_element_type=F32)
        lane = iota((16, 256), 1)
        cos_lane = lane % 32 < 16
        for n in range(8):
            own = lane // 32 == n
            c_re, s_re, c_im, s_im = (
                jnp.where(own, acc[64 * n + 16 * q:64 * n + 16 * q + 16], 0.0) for q in range(4))
            m_up, m_down, n_up, n_down = c_re + s_im, c_re - s_im, c_im - s_re, c_im + s_re
            mats[r0 + n] = jnp.concatenate(
                [jnp.where(cos_lane, m_up, n_up), jnp.where(cos_lane, m_down, n_down),
                 jnp.where(cos_lane, n_up, -m_up), jnp.where(cos_lane, n_down, -m_down)], axis=0)

    def grid_block(k, c):
        r0 = pl.multiple_of(k * run, run)

        def wait_pred(p, d):
            o = facet_peer(p)
            pred_copy(o, o, k).wait()
            return d

        lax.fori_loop(1, n_facet, wait_pred, 0)
        res_re = -vre[pl.ds(r0, run), :]
        res_im = -vim[pl.ds(r0, run), :]
        for p in range(1, n_facet):
            other = pred_all[facet_peer(p), k].astype(F32)
            res_re = res_re - other[:, :channels]
            res_im = res_im - other[:, channels:]
        for g in range(n_facet):
            share = (reader_ref[0, k] == g).astype(F32)
            seen = arrived[g].astype(F32) * share
            res_re = res_re + seen[:, :channels]
            res_im = res_im + seen[:, channels:]

        @pl.when(k == me_f)
        def _():
            resid_ref[0, :, :channels] = res_re
            resid_ref[0, :, channels:] = res_im

        h_re, h_im = hre[pl.ds(r0, run), :], him[pl.ds(r0, run), :]
        vre[pl.ds(r0, run), :] = res_re * h_re - res_im * h_im
        vim[pl.ds(r0, run), :] = res_re * h_im + res_im * h_re

        def group(i, d):
            regrid(k * (run // 8) + i)
            return d

        lax.fori_loop(0, run // 8, group, 0)
        return c

    lax.fori_loop(0, n_facet, grid_block, 0)

    ur, uc = iota((1024, 128), 0), iota((1024, 128), 1)
    unfold = jnp.where(ur // 256 == uc // 32, fold_values(uc % 32, ur % 32).astype(F32), 0.0).astype(BF16)
    spread = {}
    for lot in range(8):
        moved = [jnp.dot(perm, mats[r0:r0 + 32, 8 * lot:8 * lot + 8, :].reshape(256, 256).astype(BF16),
                         preferred_element_type=F32).astype(BF16) for r0 in range(0, R, 32)]
        for m in range(8):
            part, place_x = divmod(8 * lot + m, 32)
            x = 16 + place_x if place_x < 16 else 31 - place_x
            spread[part, x] = [got[32 * m:32 * m + 32] for got in moved]
    spread = {x: jnp.concatenate(spread[0, x] + spread[1, x], axis=0) for x in range(32)}
    out_re, out_im = [], []
    for g in range(8):
        cells = jnp.dot(jnp.concatenate([spread[4 * g + i] for i in range(4)], axis=1), unfold,
                        preferred_element_type=F32)
        g_re, g_im = cells[:R], cells[R:]
        s_re, s_im = sre[:, 128 * g:128 * g + 128], sim[:, 128 * g:128 * g + 128]
        out_re.append(((s_re * g_re + s_im * g_im) * grid_scale).astype(BF16))
        out_im.append(((s_re * g_im - s_im * g_re) * grid_scale).astype(BF16))
    both = out_re + out_im
    stacked = jnp.concatenate(
        [jnp.concatenate(both[4 * q:4 * q + 4], axis=1) for q in range(4)], axis=0)
    own_r = iota((total, 4 * R), 0)
    sub_row = jnp.sum(
        jnp.where(iota((4 * R, 4 * R), 0) == iota((4 * R, 4 * R), 1), sub_col, 0.0), axis=0, keepdims=True)
    place = (sub_row == ((own_r // chunk) * owned + own_r % owned).astype(F32)) & (
        (own_r // owned) % 4 == iota((total, 4 * R), 1) // R)
    sums = jnp.dot(place.astype(F32).astype(BF16), stacked, preferred_element_type=F32)
    part_send[...] = sums.astype(BF16).reshape(n_tile, chunk, quarter)

    def send_part(p, c):
        part_copy(tile_peer(p), me_t).start()
        return c

    lax.fori_loop(1, n_tile, send_part, 0)

    def add_part(p, acc):
        o = tile_peer(p)
        part_copy(o, o).wait()
        return acc + part_all[o].astype(F32)

    acc = lax.fori_loop(1, n_tile, add_part, part_send[me_t].astype(F32))
    for q in range(4):
        dirty_ref[0, :, q * quarter:(q + 1) * quarter] = acc[q * owned:(q + 1) * owned]


def hand_over(resid_in, dirty_in, resid_out, dirty_out):
    resid_out[...] = resid_in[...]
    dirty_out[...] = dirty_in[...]


def local(
    sectioned_rows,
    reader,
    baseline_coords,
    subgrid_index,
    stations,
    plane_index,
    model_grid,
    beam_screens,
    plane_phase,
    channel_freq,
):
    n_facet = lax.axis_size("facet")
    n_tile = lax.axis_size("tile")
    channels = channel_freq.shape[0]
    pixels = plane_phase.shape[1]
    run = sectioned_rows.shape[1]
    owned = model_grid.shape[1]
    R = n_facet * run
    chunk, quarter = 4 * owned, 2 * pixels // 4
    grid_scale = 1.0 / math.sqrt(channels * n_facet * (run * n_tile) / (owned * n_tile))

    vmem = pl.BlockSpec(memory_space=pltpu.VMEM)
    body = functools.partial(kernel, n_facet, n_tile, owned, run, channels, grid_scale)
    dma = pltpu.SemaphoreType.DMA
    resid, dirty = pl.pallas_call(
        body,
        out_shape=(
            jax.ShapeDtypeStruct((1, run, 2 * channels), F32),
            jax.ShapeDtypeStruct((1, owned, 2 * pixels), F32),
        ),
        in_specs=[pl.BlockSpec(memory_space=pltpu.SMEM)] + [vmem] * 6
        + [pl.BlockSpec(memory_space=pl.ANY)] + [vmem] * 2,
        out_specs=(vmem, vmem),
        scratch_shapes=[
            pltpu.VMEM((R, 2), F32),
            pltpu.VMEM(beam_screens.shape[1:], BF16),
            pltpu.VMEM((chunk, quarter), BF16),
            pltpu.VMEM((n_tile, chunk, quarter), BF16),
            pltpu.VMEM((n_facet, run, 2 * channels), BF16),
            pltpu.VMEM((n_facet, run, 2 * channels), BF16),
            pltpu.VMEM((n_facet, n_facet, run, 2 * channels), BF16),
            pltpu.VMEM((n_tile, chunk, quarter), BF16),
            pltpu.VMEM((n_tile, chunk, quarter), BF16),
            pltpu.VMEM((R * 32, channels), F32),
            pltpu.VMEM((R * 32, channels), BF16),
            pltpu.VMEM((R, 64, 256), F32),
            pltpu.VMEM((512, channels), BF16),
            pltpu.VMEM((R, channels), F32),
            pltpu.VMEM((R, channels), F32),
            pltpu.VMEM((R, channels), F32),
            pltpu.VMEM((R, channels), F32),
            pltpu.VMEM((R, pixels), F32),
            pltpu.VMEM((R, pixels), F32),
            dma,
            dma((n_tile,)), dma((n_tile,)),
            dma((n_facet,)), dma((n_facet,)),
            dma((n_facet, n_facet)), dma((n_facet, n_facet)),
            dma((n_tile,)), dma((n_tile,)),
        ],
        compiler_params=pltpu.CompilerParams(
            collective_id=0, has_side_effects=True, vmem_limit_bytes=60 * 1024 * 1024),
        name="predict_regrid",
    )(reader, baseline_coords, subgrid_index, stations, plane_index, sectioned_rows, model_grid,
      beam_screens[0], plane_phase, channel_freq[None, :])
    return pl.pallas_call(
        hand_over,
        out_shape=(
            jax.ShapeDtypeStruct(resid.shape, F32),
            jax.ShapeDtypeStruct(dirty.shape, F32),
        ),
        in_specs=[vmem] * 2,
        out_specs=(vmem, vmem),
        name="hand_over",
    )(resid, dirty)


def solution(mesh):
    return jax.shard_map(
        local,
        mesh=mesh,
        in_specs=(
            P("facet", "tile", None),
            P("tile", None),
            P(None, None, "tile"),
            P(None, "tile"),
            P(None, None, "tile"),
            P(None, "tile"),
            P("facet", "tile", None),
            P("facet", None, None),
            P(),
            P(),
        ),
        out_specs=(P("facet", "tile", None), P("facet", "tile", None)),
        check_vma=False,
    )
```

```python
import functools
import math

import jax
import jax.numpy as jnp
from jax import lax
from jax.experimental import pallas as pl
from jax.experimental.pallas import tpu as pltpu
from jax.sharding import PartitionSpec as P

MESH = pl.DeviceIdType.MESH
F32 = jnp.float32
BF16 = jnp.bfloat16


def cos_sin(x):
    y = x * x
    c = 1.0 / math.factorial(12)
    s = 1.0 / math.factorial(13)
    for k in range(5, -1, -1):
        sign = -1.0 if k % 2 else 1.0
        c = c * y + sign / math.factorial(2 * k)
        s = s * y + sign / math.factorial(2 * k + 1)
    return c, s * x


def iota(shape, dim):
    return lax.broadcasted_iota(jnp.int32, shape, dim)


def fold_values(cell, part_col):
    k = part_col % 16
    odd = part_col // 16
    hit = (cell == 16 + k).astype(F32)
    other = (cell == 15 - k).astype(F32)
    value = hit + other * (1.0 - 2.0 * odd.astype(F32))
    return jnp.where(part_col < 32, value, 0.0).astype(BF16)


def column(rows):
    n = rows[0].shape[1]
    diagonal = iota((n, n), 0) == iota((n, n), 1)
    return jnp.concatenate(
        [jnp.sum(jnp.where(diagonal, row.astype(F32), 0.0), axis=1, keepdims=True) for row in rows], axis=0)


def kernel(
    n_facet, n_tile, owned, run, channels, grid_scale,
    reader_ref, coords_ref, subgrid_ref, stations_ref, plane_ref, rows_ref, model_ref, screens_hbm, phase_ref, freq_ref,
    resid_ref, dirty_ref,
    cols, screens, model_send, model_all, arrived, pred_send, pred_all, part_sums, part_send, pair_recv, pair_send, part_all,
    te, tn, mats, weighted, hre, him, vre, vim, sre, sim,
    local_sem, pair_ss, pair_rs, pass_ss, pass_rs, model_ss, model_rs, vis_ss, vis_rs, pred_ss, pred_rs, part_ss, part_rs,
):
    R = n_facet * run
    me_f = lax.axis_index("facet")
    me_t = lax.axis_index("tile")
    chunk = model_send.shape[0]
    quarter = model_send.shape[1]

    load = pltpu.make_async_copy(screens_hbm, screens, local_sem)
    load.start()

    n_chip = n_tile // 2
    core = lax.rem(me_t, 2)
    chip = me_t // 2
    sibling = me_t + 1 - 2 * core

    def chip_peer(p):
        return lax.rem(chip + p, n_chip)

    def facet_peer(p):
        return lax.rem(me_f + p, n_facet)

    barrier = pltpu.get_barrier_semaphore()

    def greet_tile(p, c):
        pl.semaphore_signal(barrier, inc=1, device_id=(me_f, 2 * chip_peer(p) + core), device_id_type=MESH)
        return c

    def greet_facet(p, c):
        pl.semaphore_signal(barrier, inc=1, device_id=(facet_peer(p), me_t), device_id_type=MESH)
        return c

    pl.semaphore_signal(barrier, inc=1, device_id=(me_f, sibling), device_id_type=MESH)
    lax.fori_loop(1, n_chip, greet_tile, 0)
    lax.fori_loop(1, n_facet, greet_facet, 0)

    model_f = model_ref[0].astype(F32)
    model_send[...] = jnp.concatenate(
        [model_f[:, q * quarter:(q + 1) * quarter] for q in range(4)], axis=0
    ).astype(BF16)
    for axis in range(2):
        cols[:, axis:axis + 1] = column([coords_ref[k, axis:axis + 1, :] for k in range(n_facet)])

    pr, pc = iota((256, 256), 0), iota((256, 256), 1)
    perm = ((pr // 32 == pc % 8) & (pr % 32 == pc // 8)).astype(F32).astype(BF16)
    perm_back = ((pr // 8 == pc % 32) & (pr % 8 == pc // 32)).astype(F32).astype(BF16)
    step = 256

    def tables(axis, dst):
        def group(g, c):
            r0 = pl.multiple_of(g * 8, 8)
            at = pl.multiple_of(g * 256, 256)
            u = cols[pl.ds(r0, 8), axis:axis + 1] * (2.0 * math.pi / 64.0)
            for lo in range(0, channels, step):
                lanes = slice(lo, lo + step)
                c0, s0 = cos_sin(u * freq_ref[:, lanes])
                twice = 2.0 - 4.0 * s0 * s0
                cos_rows, sin_rows = [c0, twice * c0 - c0], [s0, twice * s0 + s0]
                for j in range(2, 16):
                    cos_rows.append(twice * cos_rows[-1] - cos_rows[-2])
                    sin_rows.append(twice * sin_rows[-1] - sin_rows[-2])
                rows = jnp.concatenate(cos_rows + sin_rows, axis=0).astype(BF16)
                moved = jnp.dot(perm, rows, preferred_element_type=F32)
                dst[pl.ds(at, 256), lanes] = moved.astype(dst.dtype)
                if axis == 0:
                    hre[pl.ds(r0, 8), lanes] = c0
                    him[pl.ds(r0, 8), lanes] = s0
                else:
                    ca, sa = hre[pl.ds(r0, 8), lanes], him[pl.ds(r0, 8), lanes]
                    hre[pl.ds(r0, 8), lanes] = ca * c0 - sa * s0
                    him[pl.ds(r0, 8), lanes] = ca * s0 + sa * c0
            return c

        lax.fori_loop(0, R // 8, group, 0)

    pl.semaphore_wait(barrier, n_chip + n_facet - 1)

    def model_copy(o, origin):
        return pltpu.make_async_remote_copy(
            src_ref=model_send, dst_ref=model_all.at[2 * origin + core], send_sem=model_ss.at[o],
            recv_sem=model_rs.at[origin], device_id=(me_f, 2 * o + core), device_id_type=MESH)

    def forward(o):
        return pltpu.make_async_remote_copy(
            src_ref=model_all.at[2 * o + core], dst_ref=model_all.at[2 * o + core], send_sem=pass_ss.at[o],
            recv_sem=pass_rs.at[o], device_id=(me_f, sibling), device_id_type=MESH)

    def passed(o):
        return pltpu.make_async_remote_copy(
            src_ref=model_all.at[2 * o + core], dst_ref=model_all.at[2 * o + 1 - core], send_sem=pass_ss.at[o],
            recv_sem=pass_rs.at[o], device_id=(me_f, sibling), device_id_type=MESH)

    def vis_copy(o, slot):
        return pltpu.make_async_remote_copy(
            src_ref=rows_ref.at[0], dst_ref=arrived.at[slot], send_sem=vis_ss.at[o],
            recv_sem=vis_rs.at[slot], device_id=(o, me_t), device_id_type=MESH)

    def pred_copy(o, slot, k):
        return pltpu.make_async_remote_copy(
            src_ref=pred_send.at[k], dst_ref=pred_all.at[slot, k], send_sem=pred_ss.at[o, k],
            recv_sem=pred_rs.at[slot, k], device_id=(o, me_t), device_id_type=MESH)

    def part_copy(o, origin):
        return pltpu.make_async_remote_copy(
            src_ref=pair_send.at[o], dst_ref=part_all.at[origin], send_sem=part_ss.at[o],
            recv_sem=part_rs.at[origin], device_id=(me_f, 2 * o + core), device_id_type=MESH)

    def send_model(p, c):
        model_copy(chip_peer(p), chip).start()
        return c

    def send_vis(p, c):
        vis_copy(facet_peer(p), me_f).start()
        return c

    lax.fori_loop(1, n_chip, send_model, 0)
    lax.fori_loop(1, n_facet, send_vis, 0)
    model_all[me_t] = model_send[...]
    forward(chip).start()
    arrived[me_f] = rows_ref[0]

    tables(0, te)
    tables(1, tn)

    def pass_on(p, c):
        o = chip_peer(p)
        model_copy(o, o).wait()
        forward(o).start()
        return c

    lax.fori_loop(1, n_chip, pass_on, 0)

    stations = screens.shape[0]
    planes, pixels = phase_ref.shape
    half_c, half_s = cos_sin(phase_ref[...] * 0.5)
    waves = jnp.concatenate([1.0 - 2.0 * half_s * half_s, 2.0 * half_s * half_c], axis=1)
    plane_hot = (column([plane_ref[k:k + 1, :] for k in range(n_facet)]) == iota((R, planes), 1).astype(F32)).astype(F32)
    wave = jnp.dot(plane_hot, waves, preferred_element_type=F32, precision=lax.Precision.HIGHEST)
    wave_re, wave_im = wave[:, :pixels], wave[:, pixels:]
    load.wait()
    pair_col = column([stations_ref[k, a:a + 1, :] for a in range(2) for k in range(n_facet)])
    station_hot = (pair_col == iota((2 * R, stations), 1).astype(F32)).astype(F32).astype(BF16)
    both_rows = jnp.dot(station_hot, screens[...], preferred_element_type=F32)
    one, two = both_rows[:R], both_rows[R:]
    one_re, one_im, two_re, two_im = one[:, :pixels], one[:, pixels:], two[:, :pixels], two[:, pixels:]
    pair_re = one_re * two_re + one_im * two_im
    pair_im = one_im * two_re - one_re * two_im
    sre[...] = pair_re * wave_re - pair_im * wave_im
    sim[...] = pair_re * wave_im + pair_im * wave_re

    def wait_passed(p, c):
        passed(chip_peer(p)).wait()
        return c

    lax.fori_loop(0, n_chip, wait_passed, 0)
    total = n_tile * chunk
    own_i = iota((4 * R, total), 1)
    sub_col = jnp.concatenate([column([subgrid_ref[k:k + 1, :] for k in range(n_facet)])] * 4, axis=0)
    pick = (sub_col == ((own_i // chunk) * owned + own_i % owned).astype(F32)) & (
        (own_i // owned) % 4 == iota((4 * R, total), 0) // R)
    found = jnp.dot(pick.astype(F32).astype(BF16), model_all[...].reshape(total, quarter),
                    preferred_element_type=F32)
    model_re = jnp.concatenate([found[:R], found[R:2 * R]], axis=1)
    model_im = jnp.concatenate([found[2 * R:3 * R], found[3 * R:]], axis=1)
    image = jnp.concatenate(
        [sre[...] * model_re - sim[...] * model_im, sre[...] * model_im + sim[...] * model_re], axis=0
    ).astype(BF16)

    fr, fc = iota((128, 1024), 0), iota((128, 1024), 1)
    fold = jnp.where(fr // 32 == fc // 256, fold_values(fr % 32, fc % 32).astype(F32), 0.0).astype(BF16)
    low = iota((R, 256), 1) % 32 < 16
    diagonal = pr // 8 % 8 == pc // 32
    by_x, folded = {}, {}
    for g in range(8):
        got = jnp.dot(image[:, 128 * g:128 * g + 128], fold, preferred_element_type=F32)
        for i in range(4):
            by_x[4 * g + i] = got[:, 256 * i:256 * i + 256]
    for j in range(16):
        up, down = by_x[16 + j], by_x[15 - j]
        even, odd = up + down, up - down
        e_re, e_im, o_re, o_im = even[:R], even[R:], odd[:R], odd[R:]
        parts = (jnp.where(low, e_re, -e_im), -jnp.where(low, o_im, o_re),
                 jnp.where(low, e_im, e_re), jnp.where(low, o_re, -o_im))
        for q in range(4):
            folded[q * 16 + j] = parts[q].astype(BF16)
    for lot in range(8):
        for r0 in range(0, R, 32):
            cells = jnp.concatenate([folded[8 * lot + m][r0:r0 + 32] for m in range(8)], axis=0)
            moved = jnp.dot(perm_back, cells, preferred_element_type=F32)
            mats[r0:r0 + 32, 8 * lot:8 * lot + 8, :] = jnp.where(diagonal, moved, 0.0).reshape(32, 8, 256)

    def degrid(g):
        r0 = pl.multiple_of(g * 8, 8)
        at = pl.multiple_of(g * 256, 256)
        lhs = mats[pl.ds(r0, 8)].reshape(512, 256).astype(BF16)
        for lo in range(0, channels, step):
            inner = jnp.dot(lhs, tn[pl.ds(at, 256), lo:lo + step], preferred_element_type=F32)
            for n in range(8):
                east = te[pl.ds(at + 32 * n, 32), lo:lo + step]
                vre[pl.ds(r0 + n, 1), lo:lo + step] = jnp.sum(
                    east * inner[64 * n:64 * n + 32], axis=0, keepdims=True)
                vim[pl.ds(r0 + n, 1), lo:lo + step] = jnp.sum(
                    east * inner[64 * n + 32:64 * n + 64], axis=0, keepdims=True)

    def predict(k, c):
        def group(i, d):
            degrid(k * (run // 8) + i)
            return d

        lax.fori_loop(0, run // 8, group, 0)
        r0 = pl.multiple_of(k * run, run)
        a_re, a_im = vre[pl.ds(r0, run), :], vim[pl.ds(r0, run), :]
        h_re, h_im = hre[pl.ds(r0, run), :], him[pl.ds(r0, run), :]
        p_re = a_re * h_re + a_im * h_im
        p_im = a_im * h_re - a_re * h_im
        vre[pl.ds(r0, run), :] = p_re
        vim[pl.ds(r0, run), :] = p_im
        pred_send[k, :, :channels] = p_re.astype(BF16)
        pred_send[k, :, channels:] = p_im.astype(BF16)

        def send_pred(p, d):
            pred_copy(facet_peer(p), me_f, k).start()
            return d

        lax.fori_loop(1, n_facet, send_pred, 0)
        return c

    lax.fori_loop(0, n_facet, predict, 0)

    def wait_vis(p, c):
        o = facet_peer(p)
        vis_copy(o, o).wait()
        return c

    lax.fori_loop(1, n_facet, wait_vis, 0)

    def regrid(g):
        r0 = pl.multiple_of(g * 8, 8)
        at = pl.multiple_of(g * 256, 256)
        for n in range(8):
            for lo in range(0, channels, step):
                east = te[pl.ds(at + 32 * n, 32), lo:lo + step]
                weighted[64 * n:64 * n + 32, lo:lo + step] = (east * vre[pl.ds(r0 + n, 1), lo:lo + step]).astype(BF16)
                weighted[64 * n + 32:64 * n + 64, lo:lo + step] = (east * vim[pl.ds(r0 + n, 1), lo:lo + step]).astype(BF16)
        acc = lax.dot_general(weighted[...], tn[pl.ds(at, 256), :], (((1,), (1,)), ((), ())),
                              preferred_element_type=F32)
        lane = iota((16, 256), 1)
        cos_lane = lane % 32 < 16
        for n in range(8):
            own = lane // 32 == n
            c_re, s_re, c_im, s_im = (
                jnp.where(own, acc[64 * n + 16 * q:64 * n + 16 * q + 16], 0.0) for q in range(4))
            m_up, m_down, n_up, n_down = c_re + s_im, c_re - s_im, c_im - s_re, c_im + s_re
            mats[r0 + n] = jnp.concatenate(
                [jnp.where(cos_lane, m_up, n_up), jnp.where(cos_lane, m_down, n_down),
                 jnp.where(cos_lane, n_up, -m_up), jnp.where(cos_lane, n_down, -m_down)], axis=0)

    def grid_block(k, c):
        r0 = pl.multiple_of(k * run, run)

        def wait_pred(p, d):
            o = facet_peer(p)
            pred_copy(o, o, k).wait()
            return d

        lax.fori_loop(1, n_facet, wait_pred, 0)
        res_re = -vre[pl.ds(r0, run), :]
        res_im = -vim[pl.ds(r0, run), :]
        for p in range(1, n_facet):
            other = pred_all[facet_peer(p), k].astype(F32)
            res_re = res_re - other[:, :channels]
            res_im = res_im - other[:, channels:]
        for g in range(n_facet):
            share = (reader_ref[0, k] == g).astype(F32)
            seen = arrived[g].astype(F32) * share
            res_re = res_re + seen[:, :channels]
            res_im = res_im + seen[:, channels:]

        @pl.when(k == me_f)
        def _():
            resid_ref[0, :, :channels] = res_re
            resid_ref[0, :, channels:] = res_im

        h_re, h_im = hre[pl.ds(r0, run), :], him[pl.ds(r0, run), :]
        vre[pl.ds(r0, run), :] = res_re * h_re - res_im * h_im
        vim[pl.ds(r0, run), :] = res_re * h_im + res_im * h_re

        def group(i, d):
            regrid(k * (run // 8) + i)
            return d

        lax.fori_loop(0, run // 8, group, 0)
        return c

    lax.fori_loop(0, n_facet, grid_block, 0)

    ur, uc = iota((1024, 128), 0), iota((1024, 128), 1)
    unfold = jnp.where(ur // 256 == uc // 32, fold_values(uc % 32, ur % 32).astype(F32), 0.0).astype(BF16)
    spread = {}
    for lot in range(8):
        moved = [jnp.dot(perm, mats[r0:r0 + 32, 8 * lot:8 * lot + 8, :].reshape(256, 256).astype(BF16),
                         preferred_element_type=F32).astype(BF16) for r0 in range(0, R, 32)]
        for m in range(8):
            part, place_x = divmod(8 * lot + m, 32)
            x = 16 + place_x if place_x < 16 else 31 - place_x
            spread[part, x] = [got[32 * m:32 * m + 32] for got in moved]
    spread = {x: jnp.concatenate(spread[0, x] + spread[1, x], axis=0) for x in range(32)}
    out_re, out_im = [], []
    for g in range(8):
        cells = jnp.dot(jnp.concatenate([spread[4 * g + i] for i in range(4)], axis=1), unfold,
                        preferred_element_type=F32)
        g_re, g_im = cells[:R], cells[R:]
        s_re, s_im = sre[:, 128 * g:128 * g + 128], sim[:, 128 * g:128 * g + 128]
        out_re.append(((s_re * g_re + s_im * g_im) * grid_scale).astype(BF16))
        out_im.append(((s_re * g_im - s_im * g_re) * grid_scale).astype(BF16))
    both = out_re + out_im
    stacked = jnp.concatenate(
        [jnp.concatenate(both[4 * q:4 * q + 4], axis=1) for q in range(4)], axis=0)
    own_r = iota((total, 4 * R), 0)
    sub_row = jnp.sum(
        jnp.where(iota((4 * R, 4 * R), 0) == iota((4 * R, 4 * R), 1), sub_col, 0.0), axis=0, keepdims=True)
    goal = own_r // chunk % n_chip * 2 + own_r // chunk // n_chip
    place = (sub_row == (goal * owned + own_r % owned).astype(F32)) & (
        (own_r // owned) % 4 == iota((total, 4 * R), 1) // R)
    sums = jnp.dot(place.astype(F32).astype(BF16), stacked, preferred_element_type=F32)
    sums = sums.reshape(n_tile, chunk, quarter)
    part_sums[...] = sums
    part_send[...] = sums.astype(BF16)
    pair_copy = pltpu.make_async_remote_copy(
        src_ref=part_send.at[pl.ds((1 - core) * n_chip, n_chip)], dst_ref=pair_recv, send_sem=pair_ss,
        recv_sem=pair_rs, device_id=(me_f, sibling), device_id_type=MESH)
    pair_copy.start()
    pair_copy.wait()
    pair_send[...] = (part_sums[pl.ds(core * n_chip, n_chip)] + pair_recv[...].astype(F32)).astype(BF16)

    def send_part(p, c):
        part_copy(chip_peer(p), chip).start()
        return c

    lax.fori_loop(1, n_chip, send_part, 0)

    def add_part(p, acc):
        o = chip_peer(p)
        part_copy(o, o).wait()
        return acc + part_all[o].astype(F32)

    own = part_sums[core * n_chip + chip] + pair_recv[chip].astype(F32)
    acc = lax.fori_loop(1, n_chip, add_part, own)
    for q in range(4):
        dirty_ref[0, :, q * quarter:(q + 1) * quarter] = acc[q * owned:(q + 1) * owned]


def hand_over(resid_in, dirty_in, resid_out, dirty_out):
    resid_out[...] = resid_in[...]
    dirty_out[...] = dirty_in[...]


def local(
    sectioned_rows,
    reader,
    baseline_coords,
    subgrid_index,
    stations,
    plane_index,
    model_grid,
    beam_screens,
    plane_phase,
    channel_freq,
):
    n_facet = lax.axis_size("facet")
    n_tile = lax.axis_size("tile")
    channels = channel_freq.shape[0]
    pixels = plane_phase.shape[1]
    run = sectioned_rows.shape[1]
    owned = model_grid.shape[1]
    R = n_facet * run
    chunk, quarter = 4 * owned, 2 * pixels // 4
    grid_scale = 1.0 / math.sqrt(channels * n_facet * (run * n_tile) / (owned * n_tile))

    vmem = pl.BlockSpec(memory_space=pltpu.VMEM)
    body = functools.partial(kernel, n_facet, n_tile, owned, run, channels, grid_scale)
    dma = pltpu.SemaphoreType.DMA
    resid, dirty = pl.pallas_call(
        body,
        out_shape=(
            jax.ShapeDtypeStruct((1, run, 2 * channels), F32),
            jax.ShapeDtypeStruct((1, owned, 2 * pixels), F32),
        ),
        in_specs=[pl.BlockSpec(memory_space=pltpu.SMEM)] + [vmem] * 6
        + [pl.BlockSpec(memory_space=pl.ANY)] + [vmem] * 2,
        out_specs=(vmem, vmem),
        scratch_shapes=[
            pltpu.VMEM((R, 2), F32),
            pltpu.VMEM(beam_screens.shape[1:], BF16),
            pltpu.VMEM((chunk, quarter), BF16),
            pltpu.VMEM((n_tile, chunk, quarter), BF16),
            pltpu.VMEM((n_facet, run, 2 * channels), BF16),
            pltpu.VMEM((n_facet, run, 2 * channels), BF16),
            pltpu.VMEM((n_facet, n_facet, run, 2 * channels), BF16),
            pltpu.VMEM((n_tile, chunk, quarter), F32),
            pltpu.VMEM((n_tile, chunk, quarter), BF16),
            pltpu.VMEM((n_tile // 2, chunk, quarter), BF16),
            pltpu.VMEM((n_tile // 2, chunk, quarter), BF16),
            pltpu.VMEM((n_tile // 2, chunk, quarter), BF16),
            pltpu.VMEM((R * 32, channels), F32),
            pltpu.VMEM((R * 32, channels), BF16),
            pltpu.VMEM((R, 64, 256), F32),
            pltpu.VMEM((512, channels), BF16),
            pltpu.VMEM((R, channels), F32),
            pltpu.VMEM((R, channels), F32),
            pltpu.VMEM((R, channels), F32),
            pltpu.VMEM((R, channels), F32),
            pltpu.VMEM((R, pixels), F32),
            pltpu.VMEM((R, pixels), F32),
            dma, dma, dma,
            dma((n_tile // 2,)), dma((n_tile // 2,)),
            dma((n_tile // 2,)), dma((n_tile // 2,)),
            dma((n_facet,)), dma((n_facet,)),
            dma((n_facet, n_facet)), dma((n_facet, n_facet)),
            dma((n_tile // 2,)), dma((n_tile // 2,)),
        ],
        compiler_params=pltpu.CompilerParams(
            collective_id=0, has_side_effects=True, vmem_limit_bytes=60 * 1024 * 1024),
        name="predict_regrid",
    )(reader, baseline_coords, subgrid_index, stations, plane_index, sectioned_rows, model_grid,
      beam_screens[0], plane_phase, channel_freq[None, :])
    return pl.pallas_call(
        hand_over,
        out_shape=(
            jax.ShapeDtypeStruct(resid.shape, F32),
            jax.ShapeDtypeStruct(dirty.shape, F32),
        ),
        in_specs=[vmem] * 2,
        out_specs=(vmem, vmem),
        name="hand_over",
    )(resid, dirty)


def solution(mesh):
    return jax.shard_map(
        local,
        mesh=mesh,
        in_specs=(
            P("facet", "tile", None),
            P("tile", None),
            P(None, None, "tile"),
            P(None, "tile"),
            P(None, None, "tile"),
            P(None, "tile"),
            P("facet", "tile", None),
            P("facet", None, None),
            P(),
            P(),
        ),
        out_specs=(P("facet", "tile", None), P("facet", "tile", None)),
        check_vma=False,
    )
```

```python
import functools
import math

import jax
import jax.numpy as jnp
from jax import lax
from jax.experimental import pallas as pl
from jax.experimental.pallas import tpu as pltpu
from jax.sharding import PartitionSpec as P

MESH = pl.DeviceIdType.MESH
F32 = jnp.float32
BF16 = jnp.bfloat16


def cos_sin(x):
    y = x * x
    c = 1.0 / math.factorial(12)
    s = 1.0 / math.factorial(13)
    for k in range(5, -1, -1):
        sign = -1.0 if k % 2 else 1.0
        c = c * y + sign / math.factorial(2 * k)
        s = s * y + sign / math.factorial(2 * k + 1)
    return c, s * x


def iota(shape, dim):
    return lax.broadcasted_iota(jnp.int32, shape, dim)


def fold_values(cell, part_col):
    k = part_col % 16
    odd = part_col // 16
    hit = (cell == 16 + k).astype(F32)
    other = (cell == 15 - k).astype(F32)
    value = hit + other * (1.0 - 2.0 * odd.astype(F32))
    return jnp.where(part_col < 32, value, 0.0).astype(BF16)


def column(rows):
    n = rows[0].shape[1]
    diagonal = iota((n, n), 0) == iota((n, n), 1)
    return jnp.concatenate(
        [jnp.sum(jnp.where(diagonal, row.astype(F32), 0.0), axis=1, keepdims=True) for row in rows], axis=0)


def kernel(
    n_facet, n_tile, owned, run, channels, grid_scale,
    reader_ref, coords_ref, subgrid_ref, stations_ref, plane_ref, rows_ref, model_ref, screens_hbm, phase_ref, freq_ref,
    resid_ref, dirty_ref,
    cols, screens, model_send, model_all, arrived, pred_send, pred_all, part_sums, part_send, pair_recv, pair_send, part_all,
    te, tn, mats, weighted, hre, him, vre, vim, sre, sim,
    local_sem, pair_ss, pair_rs, pass_ss, pass_rs, model_ss, model_rs, vis_ss, vis_rs, pred_ss, pred_rs, part_ss, part_rs,
):
    R = n_facet * run
    me_f = lax.axis_index("facet")
    me_t = lax.axis_index("tile")
    chunk = model_send.shape[0]
    quarter = model_send.shape[1]

    load = pltpu.make_async_copy(screens_hbm, screens, local_sem)
    load.start()

    n_chip = n_tile // 2
    core = lax.rem(me_t, 2)
    chip = me_t // 2
    sibling = me_t + 1 - 2 * core

    def chip_peer(p):
        return lax.rem(chip + p, n_chip)

    def facet_peer(p):
        return lax.rem(me_f + p, n_facet)

    barrier = pltpu.get_barrier_semaphore()

    def greet_tile(p, c):
        pl.semaphore_signal(barrier, inc=1, device_id=(me_f, 2 * chip_peer(p) + core), device_id_type=MESH)
        return c

    def greet_facet(p, c):
        pl.semaphore_signal(barrier, inc=1, device_id=(facet_peer(p), me_t), device_id_type=MESH)
        return c

    pl.semaphore_signal(barrier, inc=1, device_id=(me_f, sibling), device_id_type=MESH)
    lax.fori_loop(1, n_chip, greet_tile, 0)
    lax.fori_loop(1, n_facet, greet_facet, 0)

    model_f = model_ref[0].astype(F32)
    model_send[...] = jnp.concatenate(
        [model_f[:, q * quarter:(q + 1) * quarter] for q in range(4)], axis=0
    ).astype(BF16)
    for axis in range(2):
        cols[:, axis:axis + 1] = column([coords_ref[k, axis:axis + 1, :] for k in range(n_facet)])

    pr, pc = iota((256, 256), 0), iota((256, 256), 1)
    perm = ((pr // 32 == pc % 8) & (pr % 32 == pc // 8)).astype(F32).astype(BF16)
    perm_back = ((pr // 8 == pc % 32) & (pr % 8 == pc // 32)).astype(F32).astype(BF16)
    step = 256

    def tables(axis, dst):
        def group(g, c):
            r0 = pl.multiple_of(g * 8, 8)
            at = pl.multiple_of(g * 256, 256)
            u = cols[pl.ds(r0, 8), axis:axis + 1] * (2.0 * math.pi / 64.0)
            for lo in range(0, channels, step):
                lanes = slice(lo, lo + step)
                c0, s0 = cos_sin(u * freq_ref[:, lanes])
                twice = 2.0 - 4.0 * s0 * s0
                cos_rows, sin_rows = [c0, twice * c0 - c0], [s0, twice * s0 + s0]
                for j in range(2, 16):
                    cos_rows.append(twice * cos_rows[-1] - cos_rows[-2])
                    sin_rows.append(twice * sin_rows[-1] - sin_rows[-2])
                rows = jnp.concatenate(cos_rows + sin_rows, axis=0).astype(BF16)
                moved = jnp.dot(perm, rows, preferred_element_type=F32)
                dst[pl.ds(at, 256), lanes] = moved.astype(dst.dtype)
                if axis == 0:
                    hre[pl.ds(r0, 8), lanes] = c0
                    him[pl.ds(r0, 8), lanes] = s0
                else:
                    ca, sa = hre[pl.ds(r0, 8), lanes], him[pl.ds(r0, 8), lanes]
                    hre[pl.ds(r0, 8), lanes] = ca * c0 - sa * s0
                    him[pl.ds(r0, 8), lanes] = ca * s0 + sa * c0
            return c

        lax.fori_loop(0, R // 8, group, 0, unroll=2)

    pl.semaphore_wait(barrier, n_chip + n_facet - 1)

    def model_copy(o, origin):
        return pltpu.make_async_remote_copy(
            src_ref=model_send, dst_ref=model_all.at[2 * origin + core], send_sem=model_ss.at[o],
            recv_sem=model_rs.at[origin], device_id=(me_f, 2 * o + core), device_id_type=MESH)

    def forward(o):
        return pltpu.make_async_remote_copy(
            src_ref=model_all.at[2 * o + core], dst_ref=model_all.at[2 * o + core], send_sem=pass_ss.at[o],
            recv_sem=pass_rs.at[o], device_id=(me_f, sibling), device_id_type=MESH)

    def passed(o):
        return pltpu.make_async_remote_copy(
            src_ref=model_all.at[2 * o + core], dst_ref=model_all.at[2 * o + 1 - core], send_sem=pass_ss.at[o],
            recv_sem=pass_rs.at[o], device_id=(me_f, sibling), device_id_type=MESH)

    def vis_copy(o, slot):
        return pltpu.make_async_remote_copy(
            src_ref=rows_ref.at[0], dst_ref=arrived.at[slot], send_sem=vis_ss.at[o],
            recv_sem=vis_rs.at[slot], device_id=(o, me_t), device_id_type=MESH)

    def pred_copy(o, slot, k):
        return pltpu.make_async_remote_copy(
            src_ref=pred_send.at[k], dst_ref=pred_all.at[slot, k], send_sem=pred_ss.at[o, k],
            recv_sem=pred_rs.at[slot, k], device_id=(o, me_t), device_id_type=MESH)

    def part_copy(o, origin):
        return pltpu.make_async_remote_copy(
            src_ref=pair_send.at[o], dst_ref=part_all.at[origin], send_sem=part_ss.at[o],
            recv_sem=part_rs.at[origin], device_id=(me_f, 2 * o + core), device_id_type=MESH)

    def send_model(p, c):
        model_copy(chip_peer(p), chip).start()
        return c

    def send_vis(p, c):
        vis_copy(facet_peer(p), me_f).start()
        return c

    lax.fori_loop(1, n_chip, send_model, 0)
    lax.fori_loop(1, n_facet, send_vis, 0)
    model_all[me_t] = model_send[...]
    forward(chip).start()
    arrived[me_f] = rows_ref[0]

    tables(0, te)
    tables(1, tn)

    def pass_on(p, c):
        o = chip_peer(p)
        model_copy(o, o).wait()
        forward(o).start()
        return c

    lax.fori_loop(1, n_chip, pass_on, 0)

    stations = screens.shape[0]
    planes, pixels = phase_ref.shape
    half_c, half_s = cos_sin(phase_ref[...] * 0.5)
    waves = jnp.concatenate([1.0 - 2.0 * half_s * half_s, 2.0 * half_s * half_c], axis=1)
    plane_hot = (column([plane_ref[k:k + 1, :] for k in range(n_facet)]) == iota((R, planes), 1).astype(F32)).astype(F32)
    wave = jnp.dot(plane_hot, waves, preferred_element_type=F32, precision=lax.Precision.HIGHEST)
    wave_re, wave_im = wave[:, :pixels], wave[:, pixels:]
    load.wait()
    pair_col = column([stations_ref[k, a:a + 1, :] for a in range(2) for k in range(n_facet)])
    station_hot = (pair_col == iota((2 * R, stations), 1).astype(F32)).astype(F32).astype(BF16)
    both_rows = jnp.dot(station_hot, screens[...], preferred_element_type=F32)
    one, two = both_rows[:R], both_rows[R:]
    one_re, one_im, two_re, two_im = one[:, :pixels], one[:, pixels:], two[:, :pixels], two[:, pixels:]
    pair_re = one_re * two_re + one_im * two_im
    pair_im = one_im * two_re - one_re * two_im
    sre[...] = pair_re * wave_re - pair_im * wave_im
    sim[...] = pair_re * wave_im + pair_im * wave_re

    def wait_passed(p, c):
        passed(chip_peer(p)).wait()
        return c

    lax.fori_loop(0, n_chip, wait_passed, 0)
    total = n_tile * chunk
    own_i = iota((4 * R, total), 1)
    sub_col = jnp.concatenate([column([subgrid_ref[k:k + 1, :] for k in range(n_facet)])] * 4, axis=0)
    pick = (sub_col == ((own_i // chunk) * owned + own_i % owned).astype(F32)) & (
        (own_i // owned) % 4 == iota((4 * R, total), 0) // R)
    found = jnp.dot(pick.astype(F32).astype(BF16), model_all[...].reshape(total, quarter),
                    preferred_element_type=F32)
    model_re = jnp.concatenate([found[:R], found[R:2 * R]], axis=1)
    model_im = jnp.concatenate([found[2 * R:3 * R], found[3 * R:]], axis=1)
    image = jnp.concatenate(
        [sre[...] * model_re - sim[...] * model_im, sre[...] * model_im + sim[...] * model_re], axis=0
    ).astype(BF16)

    fr, fc = iota((128, 1024), 0), iota((128, 1024), 1)
    fold = jnp.where(fr // 32 == fc // 256, fold_values(fr % 32, fc % 32).astype(F32), 0.0).astype(BF16)
    low = iota((R, 256), 1) % 32 < 16
    diagonal = pr // 8 % 8 == pc // 32
    by_x, folded = {}, {}
    for g in range(8):
        got = jnp.dot(image[:, 128 * g:128 * g + 128], fold, preferred_element_type=F32)
        for i in range(4):
            by_x[4 * g + i] = got[:, 256 * i:256 * i + 256]
    for j in range(16):
        up, down = by_x[16 + j], by_x[15 - j]
        even, odd = up + down, up - down
        e_re, e_im, o_re, o_im = even[:R], even[R:], odd[:R], odd[R:]
        parts = (jnp.where(low, e_re, -e_im), -jnp.where(low, o_im, o_re),
                 jnp.where(low, e_im, e_re), jnp.where(low, o_re, -o_im))
        for q in range(4):
            folded[q * 16 + j] = parts[q].astype(BF16)
    for lot in range(8):
        for r0 in range(0, R, 32):
            cells = jnp.concatenate([folded[8 * lot + m][r0:r0 + 32] for m in range(8)], axis=0)
            moved = jnp.dot(perm_back, cells, preferred_element_type=F32)
            mats[r0:r0 + 32, 8 * lot:8 * lot + 8, :] = jnp.where(diagonal, moved, 0.0).reshape(32, 8, 256)

    def degrid(g):
        r0 = pl.multiple_of(g * 8, 8)
        at = pl.multiple_of(g * 256, 256)
        lhs = mats[pl.ds(r0, 8)].reshape(512, 256).astype(BF16)
        for lo in range(0, channels, step):
            inner = jnp.dot(lhs, tn[pl.ds(at, 256), lo:lo + step], preferred_element_type=F32)
            for n in range(8):
                east = te[pl.ds(at + 32 * n, 32), lo:lo + step]
                vre[pl.ds(r0 + n, 1), lo:lo + step] = jnp.sum(
                    east * inner[64 * n:64 * n + 32], axis=0, keepdims=True)
                vim[pl.ds(r0 + n, 1), lo:lo + step] = jnp.sum(
                    east * inner[64 * n + 32:64 * n + 64], axis=0, keepdims=True)

    def predict(k, c):
        def group(i, d):
            degrid(k * (run // 8) + i)
            return d

        lax.fori_loop(0, run // 8, group, 0, unroll=2)
        r0 = pl.multiple_of(k * run, run)
        a_re, a_im = vre[pl.ds(r0, run), :], vim[pl.ds(r0, run), :]
        h_re, h_im = hre[pl.ds(r0, run), :], him[pl.ds(r0, run), :]
        p_re = a_re * h_re + a_im * h_im
        p_im = a_im * h_re - a_re * h_im
        vre[pl.ds(r0, run), :] = p_re
        vim[pl.ds(r0, run), :] = p_im
        pred_send[k, :, :channels] = p_re.astype(BF16)
        pred_send[k, :, channels:] = p_im.astype(BF16)

        def send_pred(p, d):
            pred_copy(facet_peer(p), me_f, k).start()
            return d

        lax.fori_loop(1, n_facet, send_pred, 0)
        return c

    lax.fori_loop(0, n_facet, predict, 0)

    def wait_vis(p, c):
        o = facet_peer(p)
        vis_copy(o, o).wait()
        return c

    lax.fori_loop(1, n_facet, wait_vis, 0)

    def regrid(g):
        r0 = pl.multiple_of(g * 8, 8)
        at = pl.multiple_of(g * 256, 256)
        for n in range(8):
            for lo in range(0, channels, step):
                east = te[pl.ds(at + 32 * n, 32), lo:lo + step]
                weighted[64 * n:64 * n + 32, lo:lo + step] = (east * vre[pl.ds(r0 + n, 1), lo:lo + step]).astype(BF16)
                weighted[64 * n + 32:64 * n + 64, lo:lo + step] = (east * vim[pl.ds(r0 + n, 1), lo:lo + step]).astype(BF16)
        acc = lax.dot_general(weighted[...], tn[pl.ds(at, 256), :], (((1,), (1,)), ((), ())),
                              preferred_element_type=F32)
        lane = iota((16, 256), 1)
        cos_lane = lane % 32 < 16
        for n in range(8):
            own = lane // 32 == n
            c_re, s_re, c_im, s_im = (
                jnp.where(own, acc[64 * n + 16 * q:64 * n + 16 * q + 16], 0.0) for q in range(4))
            m_up, m_down, n_up, n_down = c_re + s_im, c_re - s_im, c_im - s_re, c_im + s_re
            mats[r0 + n] = jnp.concatenate(
                [jnp.where(cos_lane, m_up, n_up), jnp.where(cos_lane, m_down, n_down),
                 jnp.where(cos_lane, n_up, -m_up), jnp.where(cos_lane, n_down, -m_down)], axis=0)

    def grid_block(k, c):
        r0 = pl.multiple_of(k * run, run)

        def wait_pred(p, d):
            o = facet_peer(p)
            pred_copy(o, o, k).wait()
            return d

        lax.fori_loop(1, n_facet, wait_pred, 0)
        res_re = -vre[pl.ds(r0, run), :]
        res_im = -vim[pl.ds(r0, run), :]
        for p in range(1, n_facet):
            other = pred_all[facet_peer(p), k].astype(F32)
            res_re = res_re - other[:, :channels]
            res_im = res_im - other[:, channels:]
        for g in range(n_facet):
            share = (reader_ref[0, k] == g).astype(F32)
            seen = arrived[g].astype(F32) * share
            res_re = res_re + seen[:, :channels]
            res_im = res_im + seen[:, channels:]

        @pl.when(k == me_f)
        def _():
            resid_ref[0, :, :channels] = res_re
            resid_ref[0, :, channels:] = res_im

        h_re, h_im = hre[pl.ds(r0, run), :], him[pl.ds(r0, run), :]
        vre[pl.ds(r0, run), :] = res_re * h_re - res_im * h_im
        vim[pl.ds(r0, run), :] = res_re * h_im + res_im * h_re

        def group(i, d):
            regrid(k * (run // 8) + i)
            return d

        lax.fori_loop(0, run // 8, group, 0, unroll=2)
        return c

    lax.fori_loop(0, n_facet, grid_block, 0)

    ur, uc = iota((1024, 128), 0), iota((1024, 128), 1)
    unfold = jnp.where(ur // 256 == uc // 32, fold_values(uc % 32, ur % 32).astype(F32), 0.0).astype(BF16)
    spread = {}
    for lot in range(8):
        moved = [jnp.dot(perm, mats[r0:r0 + 32, 8 * lot:8 * lot + 8, :].reshape(256, 256).astype(BF16),
                         preferred_element_type=F32).astype(BF16) for r0 in range(0, R, 32)]
        for m in range(8):
            part, place_x = divmod(8 * lot + m, 32)
            x = 16 + place_x if place_x < 16 else 31 - place_x
            spread[part, x] = [got[32 * m:32 * m + 32] for got in moved]
    spread = {x: jnp.concatenate(spread[0, x] + spread[1, x], axis=0) for x in range(32)}
    out_re, out_im = [], []
    for g in range(8):
        cells = jnp.dot(jnp.concatenate([spread[4 * g + i] for i in range(4)], axis=1), unfold,
                        preferred_element_type=F32)
        g_re, g_im = cells[:R], cells[R:]
        s_re, s_im = sre[:, 128 * g:128 * g + 128], sim[:, 128 * g:128 * g + 128]
        out_re.append(((s_re * g_re + s_im * g_im) * grid_scale).astype(BF16))
        out_im.append(((s_re * g_im - s_im * g_re) * grid_scale).astype(BF16))
    both = out_re + out_im
    stacked = jnp.concatenate(
        [jnp.concatenate(both[4 * q:4 * q + 4], axis=1) for q in range(4)], axis=0)
    own_r = iota((total, 4 * R), 0)
    sub_row = jnp.sum(
        jnp.where(iota((4 * R, 4 * R), 0) == iota((4 * R, 4 * R), 1), sub_col, 0.0), axis=0, keepdims=True)
    goal = own_r // chunk % n_chip * 2 + own_r // chunk // n_chip
    place = (sub_row == (goal * owned + own_r % owned).astype(F32)) & (
        (own_r // owned) % 4 == iota((total, 4 * R), 1) // R)
    sums = jnp.dot(place.astype(F32).astype(BF16), stacked, preferred_element_type=F32)
    sums = sums.reshape(n_tile, chunk, quarter)
    part_sums[...] = sums
    part_send[...] = sums.astype(BF16)
    pair_copy = pltpu.make_async_remote_copy(
        src_ref=part_send.at[pl.ds((1 - core) * n_chip, n_chip)], dst_ref=pair_recv, send_sem=pair_ss,
        recv_sem=pair_rs, device_id=(me_f, sibling), device_id_type=MESH)
    pair_copy.start()
    pair_copy.wait()
    pair_send[...] = (part_sums[pl.ds(core * n_chip, n_chip)] + pair_recv[...].astype(F32)).astype(BF16)

    def send_part(p, c):
        part_copy(chip_peer(p), chip).start()
        return c

    lax.fori_loop(1, n_chip, send_part, 0)

    def add_part(p, acc):
        o = chip_peer(p)
        part_copy(o, o).wait()
        return acc + part_all[o].astype(F32)

    own = part_sums[core * n_chip + chip] + pair_recv[chip].astype(F32)
    acc = lax.fori_loop(1, n_chip, add_part, own)
    for q in range(4):
        dirty_ref[0, :, q * quarter:(q + 1) * quarter] = acc[q * owned:(q + 1) * owned]


def hand_over(resid_in, dirty_in, resid_out, dirty_out):
    resid_out[...] = resid_in[...]
    dirty_out[...] = dirty_in[...]


def local(
    sectioned_rows,
    reader,
    baseline_coords,
    subgrid_index,
    stations,
    plane_index,
    model_grid,
    beam_screens,
    plane_phase,
    channel_freq,
):
    n_facet = lax.axis_size("facet")
    n_tile = lax.axis_size("tile")
    channels = channel_freq.shape[0]
    pixels = plane_phase.shape[1]
    run = sectioned_rows.shape[1]
    owned = model_grid.shape[1]
    R = n_facet * run
    chunk, quarter = 4 * owned, 2 * pixels // 4
    grid_scale = 1.0 / math.sqrt(channels * n_facet * (run * n_tile) / (owned * n_tile))

    vmem = pl.BlockSpec(memory_space=pltpu.VMEM)
    body = functools.partial(kernel, n_facet, n_tile, owned, run, channels, grid_scale)
    dma = pltpu.SemaphoreType.DMA
    resid, dirty = pl.pallas_call(
        body,
        out_shape=(
            jax.ShapeDtypeStruct((1, run, 2 * channels), F32),
            jax.ShapeDtypeStruct((1, owned, 2 * pixels), F32),
        ),
        in_specs=[pl.BlockSpec(memory_space=pltpu.SMEM)] + [vmem] * 6
        + [pl.BlockSpec(memory_space=pl.ANY)] + [vmem] * 2,
        out_specs=(vmem, vmem),
        scratch_shapes=[
            pltpu.VMEM((R, 2), F32),
            pltpu.VMEM(beam_screens.shape[1:], BF16),
            pltpu.VMEM((chunk, quarter), BF16),
            pltpu.VMEM((n_tile, chunk, quarter), BF16),
            pltpu.VMEM((n_facet, run, 2 * channels), BF16),
            pltpu.VMEM((n_facet, run, 2 * channels), BF16),
            pltpu.VMEM((n_facet, n_facet, run, 2 * channels), BF16),
            pltpu.VMEM((n_tile, chunk, quarter), F32),
            pltpu.VMEM((n_tile, chunk, quarter), BF16),
            pltpu.VMEM((n_tile // 2, chunk, quarter), BF16),
            pltpu.VMEM((n_tile // 2, chunk, quarter), BF16),
            pltpu.VMEM((n_tile // 2, chunk, quarter), BF16),
            pltpu.VMEM((R * 32, channels), F32),
            pltpu.VMEM((R * 32, channels), BF16),
            pltpu.VMEM((R, 64, 256), F32),
            pltpu.VMEM((512, channels), BF16),
            pltpu.VMEM((R, channels), F32),
            pltpu.VMEM((R, channels), F32),
            pltpu.VMEM((R, channels), F32),
            pltpu.VMEM((R, channels), F32),
            pltpu.VMEM((R, pixels), F32),
            pltpu.VMEM((R, pixels), F32),
            dma, dma, dma,
            dma((n_tile // 2,)), dma((n_tile // 2,)),
            dma((n_tile // 2,)), dma((n_tile // 2,)),
            dma((n_facet,)), dma((n_facet,)),
            dma((n_facet, n_facet)), dma((n_facet, n_facet)),
            dma((n_tile // 2,)), dma((n_tile // 2,)),
        ],
        compiler_params=pltpu.CompilerParams(
            collective_id=0, has_side_effects=True, vmem_limit_bytes=60 * 1024 * 1024),
        name="predict_regrid",
    )(reader, baseline_coords, subgrid_index, stations, plane_index, sectioned_rows, model_grid,
      beam_screens[0], plane_phase, channel_freq[None, :])
    return pl.pallas_call(
        hand_over,
        out_shape=(
            jax.ShapeDtypeStruct(resid.shape, F32),
            jax.ShapeDtypeStruct(dirty.shape, F32),
        ),
        in_specs=[vmem] * 2,
        out_specs=(vmem, vmem),
        name="hand_over",
    )(resid, dirty)


def solution(mesh):
    return jax.shard_map(
        local,
        mesh=mesh,
        in_specs=(
            P("facet", "tile", None),
            P("tile", None),
            P(None, None, "tile"),
            P(None, "tile"),
            P(None, None, "tile"),
            P(None, "tile"),
            P("facet", "tile", None),
            P("facet", None, None),
            P(),
            P(),
        ),
        out_specs=(P("facet", "tile", None), P("facet", "tile", None)),
        check_vma=False,
    )
```
